512 devices in a mesh: src: 64 (over y, z), tgt: 8 (over x, core).
Axes of the slice: x: 4, y: 8, z: 8, core: 2. Of those that a mesh axis runs over, the one named last changes fastest.
Arguments:
- src_points: float32 [32, 24576], P(None, 'src'), may hold values from -14 to 14
- src_logw: float32 [24576], P('src'), may hold values from -1 to 1
- tgt_points: float32 [32, 131072], P(None, ('tgt', 'src')), may hold values from -6 to 6
- tgt_potential: float32 [1, 131072], P(None, ('tgt', 'src')), may hold values from -8 to 516
- tgt_logw: float32 [1, 131072], P(None, ('tgt', 'src')), may hold values from -1 to 1
Outputs:
- row_potential: float32 [24576], P('src')
- barycentre: float32 [32, 24576], P(None, 'src')
The draws below stay inside these ranges and needn't reach their ends.
All inputs are finite; a program needn't handle non-finite values.
Results may differ from the reference program's by a relative error of at most 0.0003.
Values sent between devices are 32-bit elements; how exact they have to be, the bound alone decides.
A program may use at most 64 MiB of HBM per device.

```python
import jax
import jax.numpy as jnp
from jax import lax

PCA = 32
SRC_DEV = 384
TGT_DEV = 256
NS = 24576
NT = 131072
N_SRC = 64


def draw_src_points(key, part):
    key = jax.random.fold_in(key, 11)
    first_key = jax.random.fold_in(key, 0)
    return jax.random.truncated_normal(first_key, -6.0, 6.0, (PCA, NS), jnp.float32)


def draw_tgt_potential(key, part):
    key = jax.random.fold_in(key, 12)
    values = jax.random.uniform(key, (1, NT), jnp.float32, -8.0, 8.0)
    return values


def block_scale(own_key, shape, shards, low, top_value):
    loudness = 1.0
    for dim, blocks in shards:
        steps = jax.random.uniform(jax.random.fold_in(jax.random.fold_in(own_key, 6), dim), (blocks,), jnp.float32, low / len(shards), top_value / len(shards))
        loudness = loudness * jnp.repeat(jnp.exp(steps), shape[dim] // blocks).reshape((-1,) + (1,) * (len(shape) - 1 - dim))
    return loudness


def bell_draw(stream_key, dims, deviation, bound, cuts=(), dtype=jnp.bfloat16):
    entries = deviation * jax.random.normal(stream_key, dims, jnp.float32)
    if cuts:
        entries = entries * block_scale(stream_key, dims, cuts, -0.22, 0.18)
    return jnp.clip(entries, -bound, bound).astype(dtype)


def setup_inputs(seed: int = 0) -> dict:
    key_of = jax.random.split(jax.random.key(seed), 6)
    src_points = draw_src_points(jax.random.fold_in(key_of[5], 71), 0)
    src_logw = jnp.clip(jax.random.uniform(key_of[1], (NS,), jnp.float32, -1.0, 1.0) * block_scale(key_of[1], (NS,), ((0, 64),), -0.4, 0.0), -1.0, 1.0)
    tgt_points = bell_draw(key_of[2], (PCA, NT), 1.0, 6.0, ((1, 512),), jnp.float32)
    tgt_potential = draw_tgt_potential(jax.random.fold_in(key_of[5], 71), 0)
    tgt_logw = jnp.clip(jax.random.uniform(key_of[4], (1, NT), jnp.float32, -1.0, 1.0) * block_scale(key_of[4], (1, NT), ((1, 512),), -0.4, 0.0), -1.0, 1.0)
    return dict(src_points=src_points, src_logw=src_logw, tgt_points=tgt_points, tgt_potential=tgt_potential, tgt_logw=tgt_logw)


entropy_scale = 4.0


def tile_scores(xblock, yblock, gblock, lblock):
    half_source = 0.5 * jnp.sum(xblock * xblock, axis=0)
    half_target = 0.5 * jnp.sum(yblock * yblock, axis=0)
    inner_product = lax.dot_general(xblock, yblock, (((0,), (0,)), ((), ())), precision=lax.Precision.HIGHEST, preferred_element_type=jnp.float32)
    transport = half_source[:, None] + half_target[None, :] - inner_product
    return (gblock[None, :] - transport) / entropy_scale + lblock[None, :]


def absorb_block(running, scores, yblock):
    row_peak, row_total, weighted = running
    new_peak = jnp.maximum(row_peak, jnp.max(scores, axis=1))
    rescale = jnp.exp(row_peak - new_peak)
    shares = jnp.exp(scores - new_peak[:, None])
    row_total = row_total * rescale + jnp.sum(shares, axis=1)
    weighted = weighted * rescale[None, :] + lax.dot_general(yblock, shares, (((1,), (1,)), ((), ())), precision=lax.Precision.HIGHEST, preferred_element_type=jnp.float32)
    return new_peak, row_total, weighted


def reference(src_points, src_logw, tgt_points, tgt_potential, tgt_logw):
    col_span = TGT_DEV * N_SRC
    col_count = NT // col_span
    row_count = NS // SRC_DEV
    target_blocks = tgt_points.reshape(PCA, col_count, col_span).transpose(1, 0, 2)
    potential_blocks = tgt_potential.reshape(col_count, col_span)
    logw_blocks = tgt_logw.reshape(col_count, col_span)
    source_blocks = src_points.reshape(PCA, row_count, SRC_DEV).transpose(1, 0, 2)

    def per_rows(xblock):
        initial = (jnp.full((SRC_DEV,), -jnp.inf, jnp.float32), jnp.zeros((SRC_DEV,), jnp.float32), jnp.zeros((PCA, SRC_DEV), jnp.float32))

        def advance(running, inputs):
            yblock, gblock, lblock = inputs
            return absorb_block(running, tile_scores(xblock, yblock, gblock, lblock), yblock), None

        final, unused = lax.scan(advance, initial, (target_blocks, potential_blocks, logw_blocks))
        return final

    peaks, totals, weighted = lax.map(per_rows, source_blocks)
    peaks = peaks.reshape(NS)
    totals = totals.reshape(NS)
    weighted = weighted.transpose(1, 0, 2).reshape(PCA, NS)
    row_potential = entropy_scale * src_logw - entropy_scale * (peaks + jnp.log(totals))
    return row_potential, weighted / totals[None, :]
```

```python
import functools
import math

import jax
import jax.numpy as jnp
from jax import lax
from jax.experimental import pallas as pl
from jax.experimental.pallas import tpu as pltpu
from jax.sharding import PartitionSpec as P

ENTROPY = 4.0
LOG2E = math.log2(math.e)
LN2 = math.log(2.0)
MESH = pl.DeviceIdType.MESH
BF16, F32 = jnp.bfloat16, jnp.float32

NY, NZ, NX, CORES = 8, 8, 4, 2
DIMS, ROWS, COLS = 32, 384, 256
TILE = 256
GROUP = 4
SHARDS = NY * CORES
BLOCKS = NZ // CORES
SPAN = GROUP * COLS
TILES = BLOCKS * ROWS // TILE
DEPTH = 256
LANES = 128
COL_TALL = 72
ROW_TALL = 104

DIRECT = {0: 0, 1: 2, 7: 3, 2: 6, 6: 7, 3: 10, 5: 11, 4: 14}
PASSED = {0: 1, 1: 4, 7: 5, 2: 8, 6: 9, 3: 12, 5: 13, 4: 15}
NEAR_FIRST = (1, 7, 2, 6, 3, 5, 4)
EVEN = (4, 2, 6, 0)
ODD = (3, 5, 1, 7)


def split(value):
    first = value.astype(BF16)
    rest = value - first.astype(F32)
    second = rest.astype(BF16)
    third = (rest - second.astype(F32)).astype(BF16)
    return first, second, third


def kernel(
    x_hbm, y_hbm, g_hbm, l_hbm, pot_ref, bary_ref,
    xown, yown, gown, lown, xraw, craw, ya, yw, xa, s0, s1, m0, m1, mrun, acc, pout, pin, xin,
    in_sem, crecv, csend, fsend, rrecv, rsend, precv, psend, xrecv, xsend,
):
    src, tgt = lax.axis_index("src"), lax.axis_index("tgt")
    yi, zi = src // NZ, src % NZ
    xi, core = tgt // CORES, tgt % CORES
    odd = (zi + core) % 2
    home = odd == 0

    def y_peer(e):
        return (((yi + e) % NY) * NZ + zi, tgt)

    def z_peer(e):
        return (yi * NZ + (zi + e) % NZ, tgt)

    def t_peer(e):
        return (src, (tgt + e) % (NX * CORES))

    sibling = (src, xi * CORES + 1 - core)

    barrier = pltpu.get_barrier_semaphore()
    for e in range(1, 8):
        pl.semaphore_signal(barrier, inc=1, device_id=y_peer(e), device_id_type=MESH)
        pl.semaphore_signal(barrier, inc=1, device_id=z_peer(e), device_id_type=MESH)
        pl.semaphore_signal(barrier, inc=1, device_id=t_peer(e), device_id_type=MESH)

    loads = [
        pltpu.make_async_copy(a, b, in_sem.at[i])
        for i, (a, b) in enumerate(((x_hbm, xown), (y_hbm, yown), (g_hbm, gown), (l_hbm, lown)))
    ]
    for load in loads:
        load.start()
    mrun[...] = jnp.full_like(mrun, -1e30)
    acc[...] = jnp.zeros_like(acc)
    for load in loads:
        load.wait()

    y = yown[...]
    bias = (gown[...] - 0.5 * jnp.sum(y * y, axis=0, keepdims=True)) * (LOG2E / ENTROPY) + lown[...] * LOG2E
    for half in range(2):
        lanes = slice(half * LANES, (half + 1) * LANES)
        craw[0, half * DIMS : (half + 1) * DIMS, :] = y[:, lanes]
    craw[0, 64:72, :] = jnp.concatenate(
        [bias[:, :LANES], bias[:, LANES:], jnp.zeros((6, LANES), F32)], axis=0
    )

    pl.semaphore_wait(barrier, 21)

    def column_copy(e):
        place = DIRECT[(8 - e) % 8]
        return pltpu.make_async_remote_copy(
            src_ref=craw.at[0], dst_ref=craw.at[place], send_sem=csend.at[e], recv_sem=crecv.at[place],
            device_id=y_peer(e), device_id_type=MESH,
        )

    def pass_copy(e):
        return pltpu.make_async_remote_copy(
            src_ref=craw.at[DIRECT[e]], dst_ref=craw.at[PASSED[e]], send_sem=fsend.at[e],
            recv_sem=crecv.at[PASSED[e]], device_id=sibling, device_id_type=MESH,
        )

    def row_copy(e):
        back = (8 - e) % 8
        slot = EVEN.index(back) if back % 2 == 0 else ODD.index(back)
        return pltpu.make_async_remote_copy(
            src_ref=xown, dst_ref=xraw.at[slot], send_sem=rsend.at[e], recv_sem=rrecv.at[slot],
            device_id=z_peer(e), device_id_type=MESH,
        )

    pass_copy(0).start()
    for e in NEAR_FIRST:
        column_copy(e).start()

    @pl.when(home)
    def _():
        for e in NEAR_FIRST:
            row_copy(e).start()

    def wait_column(place):
        pltpu.make_async_remote_copy(
            src_ref=craw.at[place], dst_ref=craw.at[place], send_sem=csend.at[0], recv_sem=crecv.at[place],
            device_id=sibling, device_id_type=MESH,
        ).wait_recv()

    def wait_rows(slot):
        pltpu.make_async_remote_copy(
            src_ref=xraw.at[slot], dst_ref=xraw.at[slot], send_sem=rsend.at[0], recv_sem=rrecv.at[slot],
            device_id=sibling, device_id_type=MESH,
        ).wait_recv()

    def prepare_rows(slot):
        x1, x2, x3 = split(xraw[slot] * (LOG2E / ENTROPY))
        row = lax.broadcasted_iota(jnp.int32, (64, ROWS), 0)
        ones = jnp.where(row < 3, 1.0, 0.0).astype(BF16)
        xa[:, slot * ROWS : (slot + 1) * ROWS] = jnp.concatenate([x1, x1, x2, x2, x1, x3, ones], axis=0)

    def prepare_columns(place):
        raw = craw[place]
        y1, y2, y3 = split(jnp.concatenate([raw[:32], raw[32:64]], axis=1))
        b = jnp.concatenate([raw[64:65], raw[65:66]], axis=1)
        b1 = b.astype(BF16).astype(F32)
        b2 = (b - b1).astype(BF16).astype(F32)
        b3 = b - b1 - b2
        row = lax.broadcasted_iota(jnp.int32, (64, COLS), 0)
        biases = jnp.where(row == 0, b1, jnp.where(row == 1, b2, jnp.where(row == 2, b3, 0.0))).astype(BF16)
        deep = jnp.concatenate([y1, y2, y1, y2, y3, y1, biases], axis=0)
        first = place * COLS if isinstance(place, int) else pl.multiple_of(place * COLS, COLS)
        ya[pl.ds(first, COLS), :] = deep.T
        yw[:, pl.ds(first, COLS)] = jnp.concatenate([y1, jnp.ones((16, COLS), BF16), y2], axis=0)

    def tile_lanes(tile):
        return pl.ds(pl.multiple_of(tile * TILE, TILE), TILE)

    def scores(group, tile, s, m):
        first = pl.multiple_of(group * SPAN, SPAN)
        value = jnp.dot(ya[pl.ds(first, SPAN), :], xa[:, tile_lanes(tile)], preferred_element_type=F32)
        s[...] = value
        m[...] = jnp.max(value.reshape(SPAN // 8, 8, TILE), axis=0)

    def absorb(group, tile, s, m):
        first = pl.multiple_of(group * SPAN, SPAN)
        lanes = tile_lanes(tile)
        old = mrun[0:1, lanes]
        new = jnp.maximum(old, jnp.max(m[...], axis=0, keepdims=True))
        mrun[0:1, lanes] = new
        share = jnp.exp2(s[...] - new)
        high = share.astype(BF16)
        low = (share - high.astype(F32)).astype(BF16)
        sums = jnp.dot(yw[:, pl.ds(first, SPAN)], high, preferred_element_type=F32)
        rest = jnp.dot(yw[0:48, pl.ds(first, SPAN)], low, preferred_element_type=F32)
        sums = jnp.concatenate([sums[:48] + rest, sums[48:]], axis=0)
        acc[:, lanes] = acc[:, lanes] * jnp.exp2(old - new) + sums

    def tile_at(step):
        group, place = step // TILES, step % TILES
        return group, jnp.where(group == 0, TILES - 1 - place, place)

    def block_offset(block):
        return EVEN[block] + odd * (ODD[block] - EVEN[block])

    def partial_copy(block):
        offset = block_offset(block)
        place = (NZ - offset) % NZ
        return pltpu.make_async_remote_copy(
            src_ref=pout.at[block], dst_ref=pin.at[place], send_sem=psend.at[block], recv_sem=precv.at[place],
            device_id=z_peer(offset), device_id_type=MESH,
        )

    def put_partial(ref, index, weighted, totals, peaks):
        for third in range(3):
            ref[index, third * DIMS : (third + 1) * DIMS, :] = weighted[third]
        ref[index, 96:104, :] = jnp.concatenate([*totals, *peaks, jnp.zeros((2, LANES), F32)], axis=0)

    def finish_block(block):
        weighted, totals, peaks = [], [], []
        for third in range(3):
            lanes = slice(block * ROWS + third * LANES, block * ROWS + (third + 1) * LANES)
            weighted.append(acc[0:32, lanes] + acc[48:80, lanes])
            totals.append(acc[32:33, lanes])
            peaks.append(mrun[0:1, lanes])
        if block < 3:
            put_partial(pout, block, weighted, totals, peaks)
            partial_copy(block).start()
        else:

            @pl.when(home)
            def _():
                put_partial(pin, 0, weighted, totals, peaks)

            @pl.when(jnp.logical_not(home))
            def _():
                put_partial(pout, block, weighted, totals, peaks)
                partial_copy(block).start()

    @pl.when(home)
    def _():
        xraw[3] = xown[...]

    @pl.when(jnp.logical_not(home))
    def _():
        wait_rows(3)

    prepare_rows(3)
    prepare_columns(0)
    wait_column(1)
    prepare_columns(1)
    for e in (1, 7):
        wait_column(DIRECT[e])
        pass_copy(e).start()
    for e in (1, 7):
        prepare_columns(DIRECT[e])
    wait_rows(2)
    prepare_rows(2)
    scores(0, TILES - 1, s0, m0)

    last = SHARDS // GROUP * TILES - 1

    def two_steps(turn, carry):
        group, third = turn // 3, turn % 3

        @pl.when(turn == 1)
        def _():
            for slot in (1, 0):
                wait_rows(slot)
                prepare_rows(slot)

        for when, passed in ((1, (2, 6)), (4, (3, 5)), (7, (4,))):

            @pl.when(turn == when)
            def _(passed=passed):
                for e in passed:
                    wait_column(DIRECT[e])
                    pass_copy(e).start()

        for when, arrived in ((2, (4, 5)), (5, (8, 9)), (8, (12, 13, 15))):

            @pl.when(turn == when)
            def _(arrived=arrived):
                for place in arrived:
                    wait_column(place)

        @pl.when(jnp.logical_and(third == 2, group < 3))
        def _():
            for place in range(GROUP):
                prepare_columns((group + 1) * GROUP + place)

        step = turn * 2
        for half, (now, now_m, later, later_m) in enumerate(((s0, m0, s1, m1), (s1, m1, s0, m0))):
            g_now, t_now = tile_at(step + half)
            g_next, t_next = tile_at(jnp.minimum(step + half + 1, last))
            scores(g_next, t_next, later, later_m)
            absorb(g_now, t_now, now, now_m)

        for when, block in ((9, 0), (10, 1)):

            @pl.when(turn == when)
            def _(block=block):
                finish_block(block)

        return carry

    lax.fori_loop(0, 12, two_steps, 0)
    finish_block(2)
    finish_block(3)

    def merge(ref, places):
        tops = [ref[place, 96:104, :] for place in places]
        peak = functools.reduce(jnp.maximum, tops)[3:6]
        factors = [jnp.exp2(top[3:6] - peak) for top in tops]
        total = functools.reduce(jnp.add, [top[0:3] * f for top, f in zip(tops, factors, strict=True)])
        weighted = []
        for third in range(3):
            rows = slice(third * DIMS, (third + 1) * DIMS)
            terms = [ref[place, rows, :] * f[third : third + 1] for place, f in zip(places, factors, strict=True)]
            weighted.append(functools.reduce(jnp.add, terms))
        return weighted, total, peak

    def sum_copy(e):
        return pltpu.make_async_remote_copy(
            src_ref=xin.at[xi], dst_ref=xin.at[xi], send_sem=xsend.at[e], recv_sem=xrecv.at[xi],
            device_id=t_peer(e), device_id_type=MESH,
        )

    def wait_sum(place):
        pltpu.make_async_remote_copy(
            src_ref=xin.at[place], dst_ref=xin.at[place], send_sem=xsend.at[0], recv_sem=xrecv.at[place],
            device_id=sibling, device_id_type=MESH,
        ).wait_recv()

    @pl.when(home)
    def _():
        for place in range(1, NZ):
            pltpu.make_async_remote_copy(
                src_ref=pin.at[place], dst_ref=pin.at[place], send_sem=psend.at[0], recv_sem=precv.at[place],
                device_id=sibling, device_id_type=MESH,
            ).wait_recv()
        weighted, total, peak = merge(pin, range(NZ))
        put_partial(xin, xi, weighted, [total], [peak])
        for e in range(1, 8):
            sum_copy(e).start()

    for place in range(1, NX):
        wait_sum((xi + place) % NX)

    @pl.when(jnp.logical_not(home))
    def _():
        wait_sum(xi)

    weighted, total, peak = merge(xin, range(NX))
    x = xown[...]
    norm = 0.5 * jnp.sum(x * x, axis=0, keepdims=True)
    for third in range(3):
        lanes = slice(third * LANES, (third + 1) * LANES)
        bary_ref[:, lanes] = weighted[third] / total[third : third + 1]
        logs = peak[third : third + 1] * LN2 + jnp.log(total[third : third + 1])
        pot_ref[:, lanes] = norm[:, lanes] - ENTROPY * logs

    for e in range(1, 8):
        column_copy(e).wait_send()
    for e in range(8):
        pass_copy(e).wait_send()
    for block in range(3):
        partial_copy(block).wait_send()

    @pl.when(home)
    def _():
        for e in range(1, 8):
            row_copy(e).wait_send()
            sum_copy(e).wait_send()

    @pl.when(jnp.logical_not(home))
    def _():
        partial_copy(3).wait_send()


def on_device(src_points, src_logw, tgt_points, tgt_potential, tgt_logw):
    dma = pltpu.SemaphoreType.DMA
    vmem = pltpu.VMEM
    potential, barycentre = pl.pallas_call(
        kernel,
        out_shape=(jax.ShapeDtypeStruct((1, ROWS), F32), jax.ShapeDtypeStruct((DIMS, ROWS), F32)),
        in_specs=[pl.BlockSpec(memory_space=pl.ANY)] * 4,
        out_specs=(pl.BlockSpec(memory_space=pltpu.VMEM),) * 2,
        scratch_shapes=[
            vmem((DIMS, ROWS), F32),
            vmem((DIMS, COLS), F32),
            vmem((1, COLS), F32),
            vmem((1, COLS), F32),
            vmem((BLOCKS, DIMS, ROWS), F32),
            vmem((SHARDS, COL_TALL, LANES), F32),
            vmem((SHARDS * COLS, DEPTH), BF16),
            vmem((80, SHARDS * COLS), BF16),
            vmem((DEPTH, BLOCKS * ROWS), BF16),
            vmem((SPAN, TILE), F32),
            vmem((SPAN, TILE), F32),
            vmem((8, TILE), F32),
            vmem((8, TILE), F32),
            vmem((8, BLOCKS * ROWS), F32),
            vmem((80, BLOCKS * ROWS), F32),
            vmem((BLOCKS, ROW_TALL, LANES), F32),
            vmem((NZ, ROW_TALL, LANES), F32),
            vmem((NX, ROW_TALL, LANES), F32),
            dma((4,)),
            dma((SHARDS,)),
            dma((8,)),
            dma((8,)),
            dma((BLOCKS,)),
            dma((8,)),
            dma((NZ,)),
            dma((BLOCKS,)),
            dma((NX,)),
            dma((8,)),
        ],
        compiler_params=pltpu.CompilerParams(
            collective_id=0, has_side_effects=True, vmem_limit_bytes=40 * 2**20
        ),
    )(src_points, tgt_points, tgt_potential, tgt_logw)
    return ENTROPY * src_logw + potential[0], barycentre


def solution(mesh):
    return jax.shard_map(
        on_device,
        mesh=mesh,
        in_specs=(
            P(None, "src"),
            P("src"),
            P(None, ("tgt", "src")),
            P(None, ("tgt", "src")),
            P(None, ("tgt", "src")),
        ),
        out_specs=(P("src"), P(None, "src")),
        check_vma=False,
    )
```

```python
import functools
import math

import jax
import jax.numpy as jnp
from jax import lax
from jax.experimental import pallas as pl
from jax.experimental.pallas import tpu as pltpu
from jax.sharding import PartitionSpec as P

ENTROPY = 4.0
LOG2E = math.log2(math.e)
LN2 = math.log(2.0)
MESH = pl.DeviceIdType.MESH
BF16, F32 = jnp.bfloat16, jnp.float32

NY, NZ, NX, CORES = 8, 8, 4, 2
DIMS, ROWS, COLS = 32, 384, 256
TILE = 256
GROUP = 4
SHARDS = NZ * CORES
BLOCKS = NY // CORES
SPAN = GROUP * COLS
TILES = BLOCKS * ROWS // TILE
DEPTH = 256
LANES = 128
COL_TALL = 72
PIECE_TALL = 40
OWNERS = ROWS // LANES

ORDER = (
    (0, 1, 2, 3, 4, 5, 6, 7),
    (1, 0, 2, 3, 4, 5, 6, 7),
    (2, 1, 3, 0, 4, 5, 6, 7),
    (3, 2, 4, 1, 0, 5, 6, 7),
    (4, 3, 5, 6, 7, 2, 1, 0),
    (5, 4, 6, 7, 3, 2, 1, 0),
    (6, 5, 7, 4, 3, 2, 1, 0),
    (7, 6, 5, 4, 3, 2, 1, 0),
)
TAKEN = (
    (-1, 0, 2, 3, 4, 5, 5),
    (-1, 0, 1, 2, 3, 3, 4),
    (-1, 0, 0, 1, 2, 2, 3),
    (-1, 0, 0, 0, 0, 1, 1),
    (-1, 0, 0, 0, 1, 1, 1),
    (-1, 0, 0, 1, 1, 1, 1),
    (-1, 0, 1, 1, 2, 2, 2),
    (-1, 1, 1, 2, 2, 2, 2),
)
NEAR_FIRST = (1, 7, 2, 6, 3, 5, 4)
EVEN = (4, 2, 6, 0)
ODD = (3, 5, 1, 7)


def split(value):
    first = value.astype(BF16)
    rest = value - first.astype(F32)
    second = rest.astype(BF16)
    third = (rest - second.astype(F32)).astype(BF16)
    return first, second, third


def kernel(
    x_hbm, y_hbm, g_hbm, l_hbm, pot_ref, bary_ref,
    xown, yown, gown, lown, xraw, craw, ya, yw, xa, s0, s1, m0, m1, mrun, acc, pout, pin, fin,
    in_sem, crecv, csend, fsend, rrecv, rsend, precv, psend, frecv, tsend, ready,
):
    src, tgt = lax.axis_index("src"), lax.axis_index("tgt")
    yi, zi = src // NZ, src % NZ
    xi, core = tgt // CORES, tgt % CORES
    odd = (yi + core) % 2
    home = odd == 0
    owner = jnp.logical_and(home, xi < OWNERS)

    def y_peer(e):
        return (((yi + e) % NY) * NZ + zi, tgt)

    def z_device(z):
        return (yi * NZ + z, tgt)

    def x_peer(e):
        return (src, ((xi + e) % NX) * CORES + core)

    def t_peer(e):
        return (src, (tgt + e) % (NX * CORES))

    sibling = (src, xi * CORES + 1 - core)

    def digits(table):
        packed = 0
        for z, row in enumerate(table):
            packed = packed + jnp.where(zi == z, sum(d * 8**i for i, d in enumerate(row)), 0)
        return [(packed // 8**i) % 8 for i in range(len(table[0]))]

    barrier = pltpu.get_barrier_semaphore()

    def greet(device):
        pl.semaphore_signal(barrier, inc=1, device_id=device, device_id_type=MESH)

    for z in range(NZ):

        @pl.when(jnp.logical_or(z > zi, z == zi - 1))
        def _(z=z):
            greet(z_device(z))

    for e in (4, 3, 5, 2, 6, 1, 7):
        if e % 2:
            greet(y_peer(e))
        else:

            @pl.when(home)
            def _(e=e):
                greet(y_peer(e))

    for e in range(1, NX):
        greet(x_peer(e))
    greet(sibling)

    loads = [
        pltpu.make_async_copy(a, b, in_sem.at[i])
        for i, (a, b) in enumerate(((x_hbm, xown), (y_hbm, yown), (g_hbm, gown), (l_hbm, lown)))
    ]
    for load in loads:
        load.start()
    mrun[...] = jnp.full_like(mrun, -1e30)
    acc[...] = jnp.zeros_like(acc)
    for load in loads:
        load.wait()

    y = yown[...]
    bias = (gown[...] - 0.5 * jnp.sum(y * y, axis=0, keepdims=True)) * (LOG2E / ENTROPY) + lown[...] * LOG2E
    for half in range(2):
        lanes = slice(half * LANES, (half + 1) * LANES)
        craw[zi, half * DIMS : (half + 1) * DIMS, :] = y[:, lanes]
    craw[zi, 64:72, :] = jnp.concatenate(
        [bias[:, :LANES], bias[:, LANES:], jnp.zeros((6, LANES), F32)], axis=0
    )

    order = digits(ORDER)
    taken = digits([[turn + 1 for turn in row] for row in TAKEN])
    pl.semaphore_wait(barrier, 7 - 3 * odd + zi + jnp.where(zi < NZ - 1, 1, 0) + NX)

    def column_copy(z):
        return pltpu.make_async_remote_copy(
            src_ref=craw.at[zi], dst_ref=craw.at[zi], send_sem=csend.at[z], recv_sem=crecv.at[zi],
            device_id=z_device(z), device_id_type=MESH,
        )

    def pass_copy(z):
        return pltpu.make_async_remote_copy(
            src_ref=craw.at[z], dst_ref=craw.at[NZ + z], send_sem=fsend.at[z], recv_sem=crecv.at[NZ + z],
            device_id=sibling, device_id_type=MESH,
        )

    def row_copy(e):
        back = (8 - e) % 8
        slot = EVEN.index(back) if back % 2 == 0 else ODD.index(back)
        return pltpu.make_async_remote_copy(
            src_ref=xown, dst_ref=xraw.at[slot], send_sem=rsend.at[e], recv_sem=rrecv.at[slot],
            device_id=y_peer(e), device_id_type=MESH,
        )

    pass_copy(zi).start()

    @pl.when(zi < NZ - 1)
    def _():
        column_copy(zi + 1).start()

    for e in range(1, NZ):

        @pl.when(zi >= e)
        def _(e=e):
            column_copy(zi - e).start()

    @pl.when(home)
    def _():
        for e in NEAR_FIRST:
            row_copy(e).start()

    def wait_column(place):
        pltpu.make_async_remote_copy(
            src_ref=craw.at[place], dst_ref=craw.at[place], send_sem=csend.at[0], recv_sem=crecv.at[place],
            device_id=sibling, device_id_type=MESH,
        ).wait_recv()

    def take(z):
        wait_column(z)
        pass_copy(z).start()

        @pl.when(z > zi + 1)
        def _():
            column_copy(z).start()

    def wait_rows(slot):
        pltpu.make_async_remote_copy(
            src_ref=xraw.at[slot], dst_ref=xraw.at[slot], send_sem=rsend.at[0], recv_sem=rrecv.at[slot],
            device_id=sibling, device_id_type=MESH,
        ).wait_recv()

    def prepare_rows(slot):
        x1, x2, x3 = split(xraw[slot] * (LOG2E / ENTROPY))
        row = lax.broadcasted_iota(jnp.int32, (64, ROWS), 0)
        ones = jnp.where(row < 3, 1.0, 0.0).astype(BF16)
        xa[:, slot * ROWS : (slot + 1) * ROWS] = jnp.concatenate([x1, x1, x2, x2, x1, x3, ones], axis=0)

    def prepare_columns(slot, place):
        raw = craw[slot]
        y1, y2, y3 = split(jnp.concatenate([raw[:32], raw[32:64]], axis=1))
        b = jnp.concatenate([raw[64:65], raw[65:66]], axis=1)
        b1 = b.astype(BF16).astype(F32)
        b2 = (b - b1).astype(BF16).astype(F32)
        b3 = b - b1 - b2
        row = lax.broadcasted_iota(jnp.int32, (64, COLS), 0)
        biases = jnp.where(row == 0, b1, jnp.where(row == 1, b2, jnp.where(row == 2, b3, 0.0))).astype(BF16)
        deep = jnp.concatenate([y1, y2, y1, y2, y3, y1, biases], axis=0)
        first = place * COLS if isinstance(place, int) else pl.multiple_of(place * COLS, COLS)
        ya[pl.ds(first, COLS), :] = deep.T
        yw[:, pl.ds(first, COLS)] = jnp.concatenate([y1, jnp.ones((16, COLS), BF16), y2], axis=0)

    def tile_lanes(tile):
        return pl.ds(pl.multiple_of(tile * TILE, TILE), TILE)

    def scores(group, tile, s, m):
        first = pl.multiple_of(group * SPAN, SPAN)
        value = jnp.dot(ya[pl.ds(first, SPAN), :], xa[:, tile_lanes(tile)], preferred_element_type=F32)
        s[...] = value
        m[...] = jnp.max(value.reshape(SPAN // 8, 8, TILE), axis=0)

    def absorb(group, tile, s, m):
        first = pl.multiple_of(group * SPAN, SPAN)
        lanes = tile_lanes(tile)
        old = mrun[0:1, lanes]
        new = jnp.maximum(old, jnp.max(m[...], axis=0, keepdims=True))
        mrun[0:1, lanes] = new
        share = jnp.exp2(s[...] - new)
        high = share.astype(BF16)
        low = (share - high.astype(F32)).astype(BF16)
        sums = jnp.dot(yw[:, pl.ds(first, SPAN)], high, preferred_element_type=F32)
        rest = jnp.dot(yw[0:48, pl.ds(first, SPAN)], low, preferred_element_type=F32)
        sums = jnp.concatenate([sums[:48] + rest, sums[48:]], axis=0)
        acc[:, lanes] = acc[:, lanes] * jnp.exp2(old - new) + sums

    def tile_at(step):
        group, place = step // TILES, step % TILES
        return group, jnp.where(group == 0, TILES - 1 - place, place)

    def block_offset(block):
        return EVEN[block] + odd * (ODD[block] - EVEN[block])

    def piece_copy(block, third):
        offset = block_offset(block)
        place = xi * NY + (NY - offset) % NY
        return pltpu.make_async_remote_copy(
            src_ref=pout.at[block * OWNERS + third], dst_ref=pin.at[place],
            send_sem=psend.at[block * OWNERS + third], recv_sem=precv.at[place],
            device_id=(((yi + offset) % NY) * NZ + zi, third * CORES + core), device_id_type=MESH,
        )

    def put_piece(ref, index, block, third):
        lanes = slice(block * ROWS + third * LANES, block * ROWS + (third + 1) * LANES)
        ref[index, 0:32, :] = acc[0:32, lanes] + acc[48:80, lanes]
        ref[index, 32:40, :] = jnp.concatenate(
            [acc[32:33, lanes], mrun[0:1, lanes], jnp.zeros((6, LANES), F32)], axis=0
        )

    def stays(block, third):
        return jnp.logical_and(block_offset(block) == 0, xi == third)

    def finish_block(block):
        for third in range(OWNERS):
            if block < 3:
                put_piece(pout, block * OWNERS + third, block, third)
                piece_copy(block, third).start()
            else:

                @pl.when(stays(block, third))
                def _(third=third):
                    put_piece(pin, xi * NY, block, third)

                @pl.when(jnp.logical_not(stays(block, third)))
                def _(third=third):
                    put_piece(pout, block * OWNERS + third, block, third)
                    piece_copy(block, third).start()

    @pl.when(home)
    def _():
        xraw[3] = xown[...]

    @pl.when(jnp.logical_not(home))
    def _():
        wait_rows(3)

    prepare_rows(3)
    first = order[1]
    take(first)
    wait_column(NZ + zi)
    prepare_columns(zi, 0)
    prepare_columns(NZ + zi, 1)
    prepare_columns(first, 2)
    wait_column(NZ + first)
    prepare_columns(NZ + first, 3)
    wait_rows(2)
    prepare_rows(2)
    scores(0, TILES - 1, s0, m0)

    last = SHARDS // GROUP * TILES - 1

    def two_steps(turn, carry):
        group, third = turn // 3, turn % 3

        @pl.when(turn == 1)
        def _():
            for slot in (1, 0):
                wait_rows(slot)
                prepare_rows(slot)
            for e in range(1, NX):
                pl.semaphore_signal(ready, inc=1, device_id=x_peer(e), device_id_type=MESH)

        for when in range(6):

            @pl.when(turn == when)
            def _(when=when):
                for i in range(1, NZ - 1):
                    if any(row[i] == when for row in TAKEN):

                        @pl.when(taken[i] == when + 1)
                        def _(i=i):
                            take(order[i + 1])

        step = turn * 2
        for half, (now, now_m, later, later_m) in enumerate(((s0, m0, s1, m1), (s1, m1, s0, m0))):
            g_now, t_now = tile_at(step + half)
            g_next, t_next = tile_at(jnp.minimum(step + half + 1, last))
            if half:
                for end in range(1, SHARDS // GROUP):

                    @pl.when(turn == 3 * end - 1)
                    def _(end=end):
                        for i in range(2):
                            z = order[2 * end + i]
                            prepare_columns(z, GROUP * end + 2 * i)
                            wait_column(NZ + z)
                            prepare_columns(NZ + z, GROUP * end + 2 * i + 1)

            scores(g_next, t_next, later, later_m)
            absorb(g_now, t_now, now, now_m)

        for when, block in ((9, 0), (10, 1)):

            @pl.when(turn == when)
            def _(block=block):
                if block == 0:
                    pl.semaphore_wait(ready, NX - 1)
                finish_block(block)

        return carry

    lax.fori_loop(0, 12, two_steps, 0)
    finish_block(2)
    finish_block(3)

    def result_copy(e):
        return pltpu.make_async_remote_copy(
            src_ref=fin.at[xi], dst_ref=fin.at[xi], send_sem=tsend.at[e], recv_sem=frecv.at[xi],
            device_id=t_peer(e), device_id_type=MESH,
        )

    @pl.when(owner)
    def _():
        for place in range(NX * NY):

            @pl.when(place != xi * NY)
            def _(place=place):
                pltpu.make_async_remote_copy(
                    src_ref=pin.at[place], dst_ref=pin.at[place], send_sem=psend.at[0], recv_sem=precv.at[place],
                    device_id=sibling, device_id_type=MESH,
                ).wait_recv()

        places = range(NX * NY)
        tops = [pin[place, 32:40, :] for place in places]
        peak = functools.reduce(jnp.maximum, tops)[1:2]
        factors = [jnp.exp2(top[1:2] - peak) for top in tops]
        total = functools.reduce(jnp.add, [top[0:1] * f for top, f in zip(tops, factors, strict=True)])
        weighted = functools.reduce(
            jnp.add, [pin[place, 0:32, :] * f for place, f in zip(places, factors, strict=True)]
        )
        fin[xi, 0:32, :] = weighted / total
        fin[xi, 32:40, :] = jnp.broadcast_to(peak * LN2 + jnp.log(total), (8, LANES))
        for e in range(1, NX * CORES):
            result_copy(e).start()

    x = xown[...]
    norm = 0.5 * jnp.sum(x * x, axis=0, keepdims=True)
    for third in range(OWNERS):

        @pl.when(jnp.logical_not(jnp.logical_and(home, xi == third)))
        def _(third=third):
            pltpu.make_async_remote_copy(
                src_ref=fin.at[third], dst_ref=fin.at[third], send_sem=tsend.at[0], recv_sem=frecv.at[third],
                device_id=sibling, device_id_type=MESH,
            ).wait_recv()

        lanes = slice(third * LANES, (third + 1) * LANES)
        bary_ref[:, lanes] = fin[third, 0:32, :]
        pot_ref[:, lanes] = norm[:, lanes] - ENTROPY * fin[third, 32:33, :]

    for z in range(NZ):

        @pl.when(zi != z)
        def _(z=z):
            column_copy(z).wait_send()

        pass_copy(z).wait_send()
    for block in range(BLOCKS):
        for third in range(OWNERS):
            if block < 3:
                piece_copy(block, third).wait_send()
            else:

                @pl.when(jnp.logical_not(stays(block, third)))
                def _(third=third):
                    piece_copy(block, third).wait_send()

    @pl.when(home)
    def _():
        for e in range(1, NY):
            row_copy(e).wait_send()

    @pl.when(owner)
    def _():
        for e in range(1, NX * CORES):
            result_copy(e).wait_send()


def on_device(src_points, src_logw, tgt_points, tgt_potential, tgt_logw):
    dma = pltpu.SemaphoreType.DMA
    vmem = pltpu.VMEM
    potential, barycentre = pl.pallas_call(
        kernel,
        out_shape=(jax.ShapeDtypeStruct((1, ROWS), F32), jax.ShapeDtypeStruct((DIMS, ROWS), F32)),
        in_specs=[pl.BlockSpec(memory_space=pl.ANY)] * 4,
        out_specs=(pl.BlockSpec(memory_space=pltpu.VMEM),) * 2,
        scratch_shapes=[
            vmem((DIMS, ROWS), F32),
            vmem((DIMS, COLS), F32),
            vmem((1, COLS), F32),
            vmem((1, COLS), F32),
            vmem((BLOCKS, DIMS, ROWS), F32),
            vmem((SHARDS, COL_TALL, LANES), F32),
            vmem((SHARDS * COLS, DEPTH), BF16),
            vmem((80, SHARDS * COLS), BF16),
            vmem((DEPTH, BLOCKS * ROWS), BF16),
            vmem((SPAN, TILE), F32),
            vmem((SPAN, TILE), F32),
            vmem((8, TILE), F32),
            vmem((8, TILE), F32),
            vmem((8, BLOCKS * ROWS), F32),
            vmem((80, BLOCKS * ROWS), F32),
            vmem((BLOCKS * OWNERS, PIECE_TALL, LANES), F32),
            vmem((NX * NY, PIECE_TALL, LANES), F32),
            vmem((OWNERS, PIECE_TALL, LANES), F32),
            dma((4,)),
            dma((SHARDS,)),
            dma((NZ,)),
            dma((NZ,)),
            dma((BLOCKS,)),
            dma((NY,)),
            dma((NX * NY,)),
            dma((BLOCKS * OWNERS,)),
            dma((OWNERS,)),
            dma((NX * CORES,)),
            pltpu.SemaphoreType.REGULAR,
        ],
        compiler_params=pltpu.CompilerParams(
            collective_id=0, has_side_effects=True, vmem_limit_bytes=63 * 2**20
        ),
    )(src_points, tgt_points, tgt_potential, tgt_logw)
    return ENTROPY * src_logw + potential[0], barycentre


def solution(mesh):
    return jax.shard_map(
        on_device,
        mesh=mesh,
        in_specs=(
            P(None, "src"),
            P("src"),
            P(None, ("tgt", "src")),
            P(None, ("tgt", "src")),
            P(None, ("tgt", "src")),
        ),
        out_specs=(P("src"), P(None, "src")),
        check_vma=False,
    )
```

```python
import functools
import math

import jax
import jax.numpy as jnp
from jax import lax
from jax.experimental import pallas as pl
from jax.experimental.pallas import tpu as pltpu
from jax.sharding import PartitionSpec as P

ENTROPY = 4.0
LOG2E = math.log2(math.e)
LN2 = math.log(2.0)
MESH = pl.DeviceIdType.MESH
BF16, F32 = jnp.bfloat16, jnp.float32

NY, NZ, NX, CORES = 8, 8, 4, 2
DIMS, ROWS, COLS = 32, 384, 256
TILE = 256
GROUP = 4
SHARDS = NZ * CORES
BLOCKS = NY // CORES
SPAN = GROUP * COLS
TILES = BLOCKS * ROWS // TILE
REST = SHARDS * COLS - 2 * SPAN
DEPTH = 256
LANES = 128
COL_TALL = 72
PIECE_TALL = 40
OWNERS = ROWS // LANES

DIRECT = {0: 0, 1: 2, 7: 3, 2: 6, 6: 7, 3: 10, 5: 11, 4: 14}
PASSED = {0: 1, 1: 4, 7: 5, 2: 8, 6: 9, 3: 12, 5: 13, 4: 15}
NEAR_FIRST = (1, 7, 2, 6, 3, 5, 4)

EVEN = (4, 2, 6, 0)
ODD = (3, 5, 1, 7)


def split(value):
    first = value.astype(BF16)
    rest = value - first.astype(F32)
    second = rest.astype(BF16)
    third = (rest - second.astype(F32)).astype(BF16)
    return first, second, third


def kernel(
    x_hbm, w_hbm, y_hbm, g_hbm, l_hbm, pot_ref, bary_ref,
    xown, wown, yown, gown, lown, xraw, craw, ya, yw, xa, s0, s1, m0, m1, mrun, acc, pout, pin, fin,
    in_sem, crecv, csend, fsend, rrecv, rsend, precv, psend, frecv, tsend, ready, ready_two,
):
    src, tgt = lax.axis_index("src"), lax.axis_index("tgt")
    yi, zi = src // NZ, src % NZ
    xi, core = tgt // CORES, tgt % CORES
    odd = (yi + core) % 2
    home = odd == 0
    owner = jnp.logical_and(core == 1, xi < OWNERS)

    def y_peer(e):
        return (((yi + e) % NY) * NZ + zi, tgt)

    def z_peer(e):
        return (yi * NZ + (zi + e) % NZ, tgt)

    def x_peer(e):
        return (src, ((xi + e) % NX) * CORES + core)

    def t_peer(e):
        return (src, (tgt + e) % (NX * CORES))

    sibling = (src, xi * CORES + 1 - core)

    barrier = pltpu.get_barrier_semaphore()

    def greet(device):
        pl.semaphore_signal(barrier, inc=1, device_id=device, device_id_type=MESH)

    for e in reversed(NEAR_FIRST):
        greet(z_peer(e))
        if e % 2:
            greet(y_peer(e))
        else:

            @pl.when(home)
            def _(e=e):
                greet(y_peer(e))

    for e in (1, NX - 1):
        greet(x_peer(e))
    greet(sibling)

    loads = [
        pltpu.make_async_copy(a, b, in_sem.at[i])
        for i, (a, b) in enumerate(((x_hbm, xown), (y_hbm, yown), (g_hbm, gown), (l_hbm, lown), (w_hbm, wown)))
    ]
    for load in loads:
        load.start()
    mrun[...] = jnp.full_like(mrun, -1e30)
    acc[...] = jnp.zeros_like(acc)
    for load in loads:
        load.wait()

    y = yown[...]
    bias = (gown[...] - 0.5 * jnp.sum(y * y, axis=0, keepdims=True)) * (LOG2E / ENTROPY) + lown[...] * LOG2E
    for half in range(2):
        lanes = slice(half * LANES, (half + 1) * LANES)
        craw[0, half * DIMS : (half + 1) * DIMS, :] = y[:, lanes]
    craw[0, 64:72, :] = jnp.concatenate(
        [bias[:, :LANES], bias[:, LANES:], jnp.zeros((6, LANES), F32)], axis=0
    )

    @pl.when(home)
    def _():
        xraw[3] = xown[...]

    pl.semaphore_wait(barrier, 17 - 3 * odd)

    def column_copy(e):
        place = DIRECT[(8 - e) % 8]
        return pltpu.make_async_remote_copy(
            src_ref=craw.at[0], dst_ref=craw.at[place], send_sem=csend.at[0], recv_sem=crecv.at[place],
            device_id=z_peer(e), device_id_type=MESH,
        )

    def pass_copy(e):
        return pltpu.make_async_remote_copy(
            src_ref=craw.at[DIRECT[e]], dst_ref=craw.at[PASSED[e]], send_sem=fsend.at[0],
            recv_sem=crecv.at[PASSED[e]], device_id=sibling, device_id_type=MESH,
        )

    def row_copy(e):
        back = (8 - e) % 8
        slot = EVEN.index(back) if back % 2 == 0 else ODD.index(back)
        return pltpu.make_async_remote_copy(
            src_ref=xown, dst_ref=xraw.at[slot], send_sem=rsend.at[e], recv_sem=rrecv.at[slot],
            device_id=y_peer(e), device_id_type=MESH,
        )

    pass_copy(0).start()
    for e in NEAR_FIRST:
        column_copy(e).start()

        @pl.when(home)
        def _(e=e):
            row_copy(e).start()

    def wait_column(place):
        pltpu.make_async_remote_copy(
            src_ref=craw.at[place], dst_ref=craw.at[place], send_sem=csend.at[0], recv_sem=crecv.at[place],
            device_id=sibling, device_id_type=MESH,
        ).wait_recv()

    def take(*places):
        for e in places:
            wait_column(DIRECT[e])
            pass_copy(e).start()

    def wait_rows(slot):
        pltpu.make_async_remote_copy(
            src_ref=xraw.at[slot], dst_ref=xraw.at[slot], send_sem=rsend.at[0], recv_sem=rrecv.at[slot],
            device_id=sibling, device_id_type=MESH,
        ).wait_recv()

    def prepare_rows(slot):
        x1, x2, x3 = split(xraw[slot] * (LOG2E / ENTROPY))
        row = lax.broadcasted_iota(jnp.int32, (64, ROWS), 0)
        ones = jnp.where(row < 3, 1.0, 0.0).astype(BF16)
        xa[:, slot * ROWS : (slot + 1) * ROWS] = jnp.concatenate([x1, x1, x2, x2, x1, x3, ones], axis=0)

    def prepare_columns(place):
        raw = craw[place]
        y1, y2, y3 = split(jnp.concatenate([raw[:32], raw[32:64]], axis=1))
        b = jnp.concatenate([raw[64:65], raw[65:66]], axis=1)
        b1 = b.astype(BF16).astype(F32)
        b2 = (b - b1).astype(BF16).astype(F32)
        b3 = b - b1 - b2
        row = lax.broadcasted_iota(jnp.int32, (64, COLS), 0)
        biases = jnp.where(row == 0, b1, jnp.where(row == 1, b2, jnp.where(row == 2, b3, 0.0))).astype(BF16)
        deep = jnp.concatenate([y1, y2, y1, y2, y3, y1, biases], axis=0)
        first = place * COLS
        ya[pl.ds(first, COLS), :] = deep.T
        yw[:, pl.ds(first, COLS)] = jnp.concatenate([y1, jnp.ones((16, COLS), BF16), y2], axis=0)

    def tile_lanes(tile):
        return pl.ds(pl.multiple_of(tile * TILE, TILE), TILE)

    def scores(first, span, tile, s, m):
        value = jnp.dot(ya[pl.ds(first, span), :], xa[:, tile_lanes(tile)], preferred_element_type=F32)
        s[0:span, :] = value
        m[...] = jnp.max(value.reshape(span // 8, 8, TILE), axis=0)

    def absorb(first, span, tile, s, m):
        lanes = tile_lanes(tile)
        old = mrun[0:1, lanes]
        new = jnp.maximum(old, jnp.max(m[...], axis=0, keepdims=True))
        mrun[0:1, lanes] = new
        share = jnp.exp2(s[0:span, :] - new)
        high = share.astype(BF16)
        low = (share - high.astype(F32)).astype(BF16)
        sums = jnp.dot(yw[:, pl.ds(first, span)], high, preferred_element_type=F32)
        rest = jnp.dot(yw[0:48, pl.ds(first, span)], low, preferred_element_type=F32)
        sums = jnp.concatenate([sums[:48] + rest, sums[48:]], axis=0)
        acc[:, lanes] = acc[:, lanes] * jnp.exp2(old - new) + sums

    def block_offset(block):
        return EVEN[block] + odd * (ODD[block] - EVEN[block])

    def piece_copy(block, third):
        offset = block_offset(block)
        place = xi * NY + (NY - offset) % NY
        return pltpu.make_async_remote_copy(
            src_ref=pout.at[block * OWNERS + third], dst_ref=pin.at[place],
            send_sem=psend.at[0], recv_sem=precv.at[0],
            device_id=(((yi + offset) % NY) * NZ + zi, third * CORES + 1), device_id_type=MESH,
        )

    def put_piece(ref, index, block, third):
        lanes = slice(block * ROWS + third * LANES, block * ROWS + (third + 1) * LANES)
        ref[index, 0:32, :] = acc[0:32, lanes] + acc[48:80, lanes]
        ref[index, 32:40, :] = jnp.concatenate(
            [acc[32:33, lanes], mrun[0:1, lanes], jnp.zeros((6, LANES), F32)], axis=0
        )

    def stays(block, third):
        return jnp.logical_and(jnp.logical_and(home, core == 1), xi == third)

    def finish_block(block):
        for third in range(OWNERS):
            if block < 3:
                put_piece(pout, block * OWNERS + third, block, third)
                piece_copy(block, third).start()
            else:

                put_piece(pout, block * OWNERS + third, block, third)

                @pl.when(stays(block, third))
                def _(third=third):
                    pltpu.make_async_copy(
                        pout.at[block * OWNERS + third], pin.at[xi * NY], precv.at[0]
                    ).start()

                @pl.when(jnp.logical_not(stays(block, third)))
                def _(third=third):
                    piece_copy(block, third).start()

    def prepare_group(group):
        for place in range(group * GROUP, (group + 1) * GROUP):
            if place > 0 and place not in (2, 3, 6, 7, 10, 11, 14):
                wait_column(place)
            prepare_columns(place)

    def take_rows(slot):
        wait_rows(slot)
        prepare_rows(slot)

    @pl.when(home)
    def _():
        prepare_rows(3)

    @pl.when(jnp.logical_not(home))
    def _():
        take_rows(3)

    take(1, 7)
    prepare_group(0)

    scores(0, SPAN, 5, s0, m0)
    take_rows(2)
    scores(0, SPAN, 4, s1, m1)
    absorb(0, SPAN, 5, s0, m0)
    take(2, 6)
    scores(0, SPAN, 3, s0, m0)
    absorb(0, SPAN, 4, s1, m1)
    take_rows(1)
    scores(0, SPAN, 2, s1, m1)
    absorb(0, SPAN, 3, s0, m0)
    take_rows(0)
    for e in (1, NX - 1):
        pl.semaphore_signal(ready, inc=1, device_id=x_peer(e), device_id_type=MESH)
    scores(0, SPAN, 1, s0, m0)
    absorb(0, SPAN, 2, s1, m1)
    take(3, 5)
    scores(0, SPAN, 0, s1, m1)
    absorb(0, SPAN, 1, s0, m0)
    prepare_group(1)

    scores(SPAN, SPAN, 0, s0, m0)
    absorb(0, SPAN, 0, s1, m1)
    take(4)
    for tile in range(0, TILES - 2, 2):
        scores(SPAN, SPAN, tile + 1, s1, m1)
        absorb(SPAN, SPAN, tile, s0, m0)
        scores(SPAN, SPAN, tile + 2, s0, m0)
        absorb(SPAN, SPAN, tile + 1, s1, m1)
    scores(SPAN, SPAN, TILES - 1, s1, m1)
    absorb(SPAN, SPAN, TILES - 2, s0, m0)
    for group in range(2, SHARDS // GROUP):
        prepare_group(group)
    pl.semaphore_wait(ready, 2)
    for e in (1, NX - 1):
        pl.semaphore_signal(ready_two, inc=1, device_id=x_peer(e), device_id_type=MESH)

    rest = 2 * SPAN
    scores(rest, REST, 0, s0, m0)
    absorb(SPAN, SPAN, TILES - 1, s1, m1)

    def two_tiles(turn, carry):
        scores(rest, REST, 2 * turn + 1, s1, m1)
        absorb(rest, REST, 2 * turn, s0, m0)

        @pl.when(turn == 1)
        def _():
            finish_block(1)

        scores(rest, REST, 2 * turn + 2, s0, m0)
        absorb(rest, REST, 2 * turn + 1, s1, m1)

        @pl.when(turn == 0)
        def _():
            pl.semaphore_wait(ready_two, 2)
            finish_block(0)

        return carry

    lax.fori_loop(0, 2, two_tiles, 0)
    scores(rest, REST, TILES - 1, s1, m1)
    absorb(rest, REST, TILES - 2, s0, m0)
    finish_block(2)
    absorb(rest, REST, TILES - 1, s1, m1)
    finish_block(3)

    def result_copy(e):
        return pltpu.make_async_remote_copy(
            src_ref=fin.at[xi], dst_ref=fin.at[xi], send_sem=tsend.at[0], recv_sem=frecv.at[xi],
            device_id=t_peer(e), device_id_type=MESH,
        )

    @pl.when(owner)
    def _():
        pltpu.make_async_copy(pin, pin, precv.at[0]).wait()
        places = range(NX * NY)
        tops = [pin[place, 32:40, :] for place in places]
        peak = functools.reduce(jnp.maximum, tops)[1:2]
        factors = [jnp.exp2(top[1:2] - peak) for top in tops]
        total = functools.reduce(jnp.add, [top[0:1] * f for top, f in zip(tops, factors, strict=True)])
        weighted = functools.reduce(
            jnp.add, [pin[place, 0:32, :] * f for place, f in zip(places, factors, strict=True)]
        )
        fin[xi, 0:32, :] = weighted / total
        fin[xi, 32:40, :] = jnp.broadcast_to(peak * LN2 + jnp.log(total), (8, LANES))
        for e in (4, 3, 5, 2, 6, 1, 7):
            result_copy(e).start()

    x = xown[...]
    norm = 0.5 * jnp.sum(x * x, axis=0, keepdims=True)
    for third in range(OWNERS):

        @pl.when(jnp.logical_not(jnp.logical_and(core == 1, xi == third)))
        def _(third=third):
            pltpu.make_async_remote_copy(
                src_ref=fin.at[third], dst_ref=fin.at[third], send_sem=tsend.at[0], recv_sem=frecv.at[third],
                device_id=sibling, device_id_type=MESH,
            ).wait_recv()

        lanes = slice(third * LANES, (third + 1) * LANES)
        bary_ref[:, lanes] = fin[third, 0:32, :]
        pot_ref[lanes] = ENTROPY * wown[lanes] + (norm[:, lanes] - ENTROPY * fin[third, 32:33, :]).reshape(LANES)

    def wait_sent(ref, sem):
        pltpu.make_async_remote_copy(
            src_ref=ref, dst_ref=ref, send_sem=sem, recv_sem=crecv.at[0], device_id=sibling, device_id_type=MESH
        ).wait_send()

    wait_sent(craw.at[pl.ds(0, NZ - 1)], csend.at[0])
    wait_sent(craw.at[pl.ds(0, NZ)], fsend.at[0])
    keeps = jnp.logical_and(home, owner)

    @pl.when(keeps)
    def _():
        wait_sent(pout.at[pl.ds(0, BLOCKS * OWNERS - 1)], psend.at[0])

    @pl.when(jnp.logical_not(keeps))
    def _():
        wait_sent(pout, psend.at[0])

    @pl.when(home)
    def _():
        for e in range(1, NY):
            row_copy(e).wait_send()

    @pl.when(owner)
    def _():
        wait_sent(pin.at[pl.ds(0, NX * CORES - 1)], tsend.at[0])


def hand_over(pot_in, bary_in, pot_out, bary_out):
    pot_out[...] = pot_in[...]
    bary_out[...] = bary_in[...]


def on_device(src_points, src_logw, tgt_points, tgt_potential, tgt_logw):
    dma = pltpu.SemaphoreType.DMA
    vmem = pltpu.VMEM
    shapes = (jax.ShapeDtypeStruct((ROWS,), F32), jax.ShapeDtypeStruct((DIMS, ROWS), F32))
    results = pl.pallas_call(
        kernel,
        out_shape=shapes,
        in_specs=[pl.BlockSpec(memory_space=pl.ANY)] * 5,
        out_specs=(pl.BlockSpec(memory_space=vmem),) * 2,
        scratch_shapes=[
            vmem((DIMS, ROWS), F32),
            vmem((ROWS,), F32),
            vmem((DIMS, COLS), F32),
            vmem((1, COLS), F32),
            vmem((1, COLS), F32),
            vmem((BLOCKS, DIMS, ROWS), F32),
            vmem((SHARDS, COL_TALL, LANES), F32),
            vmem((SHARDS * COLS, DEPTH), BF16),
            vmem((80, SHARDS * COLS), BF16),
            vmem((DEPTH, BLOCKS * ROWS), BF16),
            vmem((REST, TILE), F32),
            vmem((REST, TILE), F32),
            vmem((8, TILE), F32),
            vmem((8, TILE), F32),
            vmem((8, BLOCKS * ROWS), F32),
            vmem((80, BLOCKS * ROWS), F32),
            vmem((BLOCKS * OWNERS, PIECE_TALL, LANES), F32),
            vmem((NX * NY, PIECE_TALL, LANES), F32),
            vmem((OWNERS, PIECE_TALL, LANES), F32),
            dma((5,)),
            dma((SHARDS,)),
            dma((1,)),
            dma((1,)),
            dma((BLOCKS,)),
            dma((NY,)),
            dma((1,)),
            dma((1,)),
            dma((OWNERS,)),
            dma((1,)),
            pltpu.SemaphoreType.REGULAR,
            pltpu.SemaphoreType.REGULAR,
        ],
        compiler_params=pltpu.CompilerParams(
            collective_id=0, has_side_effects=True, vmem_limit_bytes=63 * 2**20
        ),
    )(src_points, src_logw, tgt_points, tgt_potential, tgt_logw)
    return pl.pallas_call(
        hand_over,
        out_shape=shapes,
        in_specs=[pl.BlockSpec(memory_space=vmem)] * 2,
        out_specs=(pl.BlockSpec(memory_space=vmem),) * 2,
    )(*results)


def solution(mesh):
    return jax.shard_map(
        on_device,
        mesh=mesh,
        in_specs=(
            P(None, "src"),
            P("src"),
            P(None, ("tgt", "src")),
            P(None, ("tgt", "src")),
            P(None, ("tgt", "src")),
        ),
        out_specs=(P("src"), P(None, "src")),
        check_vma=False,
    )
```

```python
import functools
import math

import jax
import jax.numpy as jnp
from jax import lax
from jax.experimental import pallas as pl
from jax.experimental.pallas import tpu as pltpu
from jax.sharding import PartitionSpec as P

ENTROPY = 4.0
LOG2E = math.log2(math.e)
LN2 = math.log(2.0)
MESH = pl.DeviceIdType.MESH
BF16, F32 = jnp.bfloat16, jnp.float32

NY, NZ, NX, CORES = 8, 8, 4, 2
DIMS, ROWS, COLS = 32, 384, 256
TILE = 256
GROUP = 4
SHARDS = NZ * CORES
BLOCKS = NY // CORES
SPAN = GROUP * COLS
TILES = BLOCKS * ROWS // TILE
REST = SHARDS * COLS - 2 * SPAN
DEPTH = 256
LANES = 128
COL_TALL = 72
PIECE_TALL = 40
OWNERS = ROWS // LANES

COLUMNS = (0, 8, 1, 2, 9, 10, 3, 11, 4, 12, 5, 13, 6, 14, 7, 15)
SPOT = {place: spot for spot, place in enumerate(COLUMNS)}
LOW = 4

NEAR = (1, 7)
FAR = (2, 6, 3, 5)

EVEN = (4, 2, 6, 0)
ODD = (3, 5, 1, 7)


def split(value):
    first = value.astype(BF16)
    rest = value - first.astype(F32)
    second = rest.astype(BF16)
    third = (rest - second.astype(F32)).astype(BF16)
    return first, second, third


def kernel(
    x_hbm, w_hbm, y_hbm, g_hbm, l_hbm, pot_ref, bary_ref,
    xown, wown, yown, gown, lown, xraw, craw, ya, yw, xa, s0, s1, m0, m1, mrun, acc, pout, pin, fin,
    in_sem, crecv, csend, fsend, rrecv, rsend, precv, psend, frecv, tsend, ready, ready_two, later_in,
):
    src, tgt = lax.axis_index("src"), lax.axis_index("tgt")
    yi, zi = src // NZ, src % NZ
    xi, core = tgt // CORES, tgt % CORES
    odd = (yi + core) % 2
    home = odd == 0
    low = zi < LOW
    owner = jnp.logical_and(core == 1, xi < OWNERS)

    def y_peer(e):
        return (((yi + e) % NY) * NZ + zi, tgt)

    def z_peer(tie):
        bits = [(zi // 2**i) % 2 for i in range(3)]
        z = sum((1 - bit if tie // 2**i % 2 else bit) * 2**i for i, bit in enumerate(bits))
        return (yi * NZ + z, tgt)

    def x_peer(e):
        return (src, ((xi + e) % NX) * CORES + core)

    def t_peer(e):
        return (src, (tgt + e) % (NX * CORES))

    sibling = (src, xi * CORES + 1 - core)

    barrier = pltpu.get_barrier_semaphore()

    def greet(device):
        pl.semaphore_signal(barrier, inc=1, device_id=device, device_id_type=MESH)

    @pl.when(low)
    def _():
        for tie in range(LOW, NZ):
            greet(z_peer(tie))

    for tie in (3, 2, 1):
        greet(z_peer(tie))
    for e in reversed(NEAR + FAR):
        if e % 2:
            greet(y_peer(e))
        else:

            @pl.when(home)
            def _(e=e):
                greet(y_peer(e))

    for e in (1, NX - 1):
        greet(x_peer(e))
    greet(sibling)

    loads = [
        pltpu.make_async_copy(a, b, in_sem.at[i])
        for i, (a, b) in enumerate(((x_hbm, xown), (y_hbm, yown), (g_hbm, gown), (l_hbm, lown), (w_hbm, wown)))
    ]
    for load in loads:
        load.start()
    mrun[...] = jnp.full_like(mrun, -1e30)
    acc[...] = jnp.zeros_like(acc)
    for load in loads:
        load.wait()

    y = yown[...]
    bias = (gown[...] - 0.5 * jnp.sum(y * y, axis=0, keepdims=True)) * (LOG2E / ENTROPY) + lown[...] * LOG2E
    for half in range(2):
        lanes = slice(half * LANES, (half + 1) * LANES)
        craw[0, half * DIMS : (half + 1) * DIMS, :] = y[:, lanes]
    craw[0, 64:72, :] = jnp.concatenate(
        [bias[:, :LANES], bias[:, LANES:], jnp.zeros((6, LANES), F32)], axis=0
    )

    @pl.when(home)
    def _():
        xraw[3] = xown[...]

    pl.semaphore_wait(barrier, 16 - 2 * odd - 4 * jnp.where(low, 1, 0))

    def column_copy(tie):
        return pltpu.make_async_remote_copy(
            src_ref=craw.at[0], dst_ref=craw.at[tie], send_sem=csend.at[0], recv_sem=crecv.at[tie],
            device_id=z_peer(tie), device_id_type=MESH,
        )

    def pass_copy(tie):
        return pltpu.make_async_remote_copy(
            src_ref=craw.at[tie], dst_ref=craw.at[NZ + tie], send_sem=fsend.at[0],
            recv_sem=crecv.at[NZ + tie], device_id=sibling, device_id_type=MESH,
        )

    def row_copy(e):
        back = (8 - e) % 8
        slot = EVEN.index(back) if back % 2 == 0 else ODD.index(back)
        return pltpu.make_async_remote_copy(
            src_ref=xown, dst_ref=xraw.at[slot], send_sem=rsend.at[e], recv_sem=rrecv.at[slot],
            device_id=y_peer(e), device_id_type=MESH,
        )

    def last_row_copy():
        return pltpu.make_async_remote_copy(
            src_ref=xraw.at[0], dst_ref=xraw.at[0], send_sem=rsend.at[4], recv_sem=rrecv.at[0],
            device_id=y_peer(7), device_id_type=MESH,
        )

    def send_rows(places):
        @pl.when(home)
        def _():
            for e in places:
                row_copy(e).start()

    def across():
        for tie in range(LOW, NZ):
            column_copy(tie).start()

    def wait_column(place):
        pltpu.make_async_remote_copy(
            src_ref=craw.at[place], dst_ref=craw.at[place], send_sem=csend.at[0], recv_sem=crecv.at[place],
            device_id=sibling, device_id_type=MESH,
        ).wait_recv()

    def take(*ties):
        for tie in ties:
            wait_column(tie)
            pass_copy(tie).start()

    def wait_rows(slot):
        pltpu.make_async_remote_copy(
            src_ref=xraw.at[slot], dst_ref=xraw.at[slot], send_sem=rsend.at[0], recv_sem=rrecv.at[slot],
            device_id=sibling, device_id_type=MESH,
        ).wait_recv()

    def prepare_rows(slot):
        x1, x2, x3 = split(xraw[slot] * (LOG2E / ENTROPY))
        row = lax.broadcasted_iota(jnp.int32, (64, ROWS), 0)
        ones = jnp.where(row < 3, 1.0, 0.0).astype(BF16)
        xa[:, slot * ROWS : (slot + 1) * ROWS] = jnp.concatenate([x1, x1, x2, x2, x1, x3, ones], axis=0)

    def prepare_columns(place):
        raw = craw[place]
        y1, y2, y3 = split(jnp.concatenate([raw[:32], raw[32:64]], axis=1))
        b = jnp.concatenate([raw[64:65], raw[65:66]], axis=1)
        b1 = b.astype(BF16).astype(F32)
        b2 = (b - b1).astype(BF16).astype(F32)
        b3 = b - b1 - b2
        row = lax.broadcasted_iota(jnp.int32, (64, COLS), 0)
        biases = jnp.where(row == 0, b1, jnp.where(row == 1, b2, jnp.where(row == 2, b3, 0.0))).astype(BF16)
        deep = jnp.concatenate([y1, y2, y1, y2, y3, y1, biases], axis=0)
        first = SPOT[place] * COLS
        ya[pl.ds(first, COLS), :] = deep.T
        yw[:, pl.ds(first, COLS)] = jnp.concatenate([y1, jnp.ones((16, COLS), BF16), y2], axis=0)

    def tile_lanes(tile):
        return pl.ds(pl.multiple_of(tile * TILE, TILE), TILE)

    def scores(first, span, tile, s, m):
        value = jnp.dot(ya[pl.ds(first, span), :], xa[:, tile_lanes(tile)], preferred_element_type=F32)
        s[0:span, :] = value
        m[...] = jnp.max(value.reshape(span // 8, 8, TILE), axis=0)

    def absorb(first, span, tile, s, m):
        lanes = tile_lanes(tile)
        old = mrun[0:1, lanes]
        new = jnp.maximum(old, jnp.max(m[...], axis=0, keepdims=True))
        mrun[0:1, lanes] = new
        share = jnp.exp2(s[0:span, :] - new)
        high = share.astype(BF16)
        low = (share - high.astype(F32)).astype(BF16)
        sums = jnp.dot(yw[:, pl.ds(first, span)], high, preferred_element_type=F32)
        rest = jnp.dot(yw[0:48, pl.ds(first, span)], low, preferred_element_type=F32)
        sums = jnp.concatenate([sums[:48] + rest, sums[48:]], axis=0)
        acc[:, lanes] = acc[:, lanes] * jnp.exp2(old - new) + sums

    def block_offset(block):
        return EVEN[block] + odd * (ODD[block] - EVEN[block])

    def piece_copy(block, third):
        offset = block_offset(block)
        place = xi * NY + (NY - offset) % NY
        return pltpu.make_async_remote_copy(
            src_ref=pout.at[block * OWNERS + third], dst_ref=pin.at[place],
            send_sem=psend.at[0], recv_sem=precv.at[0],
            device_id=(((yi + offset) % NY) * NZ + zi, third * CORES + 1), device_id_type=MESH,
        )

    def put_piece(ref, index, block, third):
        lanes = slice(block * ROWS + third * LANES, block * ROWS + (third + 1) * LANES)
        ref[index, 0:32, :] = acc[0:32, lanes] + acc[48:80, lanes]
        ref[index, 32:40, :] = jnp.concatenate(
            [acc[32:33, lanes], mrun[0:1, lanes], jnp.zeros((6, LANES), F32)], axis=0
        )

    def stays(block, third):
        return jnp.logical_and(jnp.logical_and(home, core == 1), xi == third)

    def finish_tile(tile):
        for unit in range(tile * TILE // LANES, (tile + 1) * TILE // LANES):
            block, third = unit // OWNERS, unit % OWNERS
            put_piece(pout, unit, block, third)
            if block < 3:
                piece_copy(block, third).start()
            else:

                @pl.when(stays(block, third))
                def _(unit=unit):
                    pltpu.make_async_copy(pout.at[unit], pin.at[xi * NY], precv.at[0]).start()

                @pl.when(jnp.logical_not(stays(block, third)))
                def _(block=block, third=third):
                    piece_copy(block, third).start()

    def prepare(*places):
        for place in places:
            prepare_columns(place)

    def arrived(*ties):
        for tie in ties:
            wait_column(NZ + tie)

    def take_rows(slot):
        wait_rows(slot)
        prepare_rows(slot)

    pass_copy(0).start()
    column_copy(1).start()
    send_rows(NEAR)

    @pl.when(jnp.logical_not(low))
    def _():
        across()
        for tie in range(LOW, NZ):
            pl.semaphore_signal(later_in, inc=1, device_id=z_peer(tie), device_id_type=MESH)

    column_copy(2).start()
    prepare(0)

    @pl.when(home)
    def _():
        prepare_rows(3)

    column_copy(3).start()
    send_rows(FAR)

    @pl.when(jnp.logical_not(home))
    def _():
        take_rows(3)

    arrived(0)
    take(1, 2)
    prepare(8, 1, 2)

    buffers = ((s0, m0), (s1, m1))

    def step(number, done, following):
        if following is not None:
            scores(*following, *buffers[(number + 1) % 2])
        if done is not None:
            absorb(*done, *buffers[number % 2])

    one, two, rest = (0, SPAN), (SPAN, SPAN), (2 * SPAN, REST)

    step(-1, None, (*one, 5))
    take_rows(2)
    step(0, (*one, 5), (*one, 4))
    take(3)
    step(1, (*one, 4), (*one, 3))
    take_rows(1)

    @pl.when(jnp.logical_not(home))
    def _():
        wait_rows(0)
        last_row_copy().start()
        prepare_rows(0)

    step(2, (*one, 3), (*one, 2))
    arrived(1, 2, 3)
    prepare(9, 10, 3, 11)
    step(3, (*one, 2), (*two, 5))

    @pl.when(low)
    def _():
        pl.semaphore_wait(later_in, NZ - LOW)
        across()

    step(4, (*two, 5), (*two, 4))
    step(5, (*two, 4), (*two, 3))
    step(6, (*two, 3), (*two, 2))

    @pl.when(home)
    def _():
        take_rows(0)

    for e in (1, NX - 1):
        pl.semaphore_signal(ready, inc=1, device_id=x_peer(e), device_id_type=MESH)
    step(7, (*two, 2), (*one, 1))
    step(8, (*one, 1), (*one, 0))
    take(7, 6, 5, 4)
    prepare(7, 6, 5, 4)
    step(9, (*one, 0), (*two, 1))
    pl.semaphore_wait(ready, 2)
    for e in (1, NX - 1):
        pl.semaphore_signal(ready_two, inc=1, device_id=x_peer(e), device_id_type=MESH)
    step(10, (*two, 1), (*two, 0))
    arrived(7, 6, 5, 4)
    prepare(15, 14, 13, 12)

    step(11, (*two, 0), (*rest, 0))

    def two_tiles(turn, carry):
        scores(*rest, 2 * turn + 1, s1, m1)
        absorb(*rest, 2 * turn, s0, m0)
        for when in range(2):

            @pl.when(turn == when)
            def _(when=when):
                if when == 0:
                    pl.semaphore_wait(ready_two, 2)
                finish_tile(2 * when)

        scores(*rest, 2 * turn + 2, s0, m0)
        absorb(*rest, 2 * turn + 1, s1, m1)
        for when in range(2):

            @pl.when(turn == when)
            def _(when=when):
                finish_tile(2 * when + 1)

        return carry

    lax.fori_loop(0, 2, two_tiles, 0)
    scores(*rest, TILES - 1, s1, m1)
    absorb(*rest, TILES - 2, s0, m0)
    finish_tile(TILES - 2)
    absorb(*rest, TILES - 1, s1, m1)
    finish_tile(TILES - 1)

    def result_copy(e):
        return pltpu.make_async_remote_copy(
            src_ref=fin.at[xi], dst_ref=fin.at[xi], send_sem=tsend.at[0], recv_sem=frecv.at[xi],
            device_id=t_peer(e), device_id_type=MESH,
        )

    @pl.when(owner)
    def _():
        pltpu.make_async_copy(pin, pin, precv.at[0]).wait()
        places = range(NX * NY)
        tops = [pin[place, 32:40, :] for place in places]
        peak = functools.reduce(jnp.maximum, tops)[1:2]
        factors = [jnp.exp2(top[1:2] - peak) for top in tops]
        total = functools.reduce(jnp.add, [top[0:1] * f for top, f in zip(tops, factors, strict=True)])
        weighted = functools.reduce(
            jnp.add, [pin[place, 0:32, :] * f for place, f in zip(places, factors, strict=True)]
        )
        fin[xi, 0:32, :] = weighted / total
        fin[xi, 32:40, :] = jnp.broadcast_to(peak * LN2 + jnp.log(total), (8, LANES))
        for e in (4, 3, 5, 2, 6, 1, 7):
            result_copy(e).start()

    x = xown[...]
    norm = 0.5 * jnp.sum(x * x, axis=0, keepdims=True)
    for third in range(OWNERS):

        @pl.when(jnp.logical_not(jnp.logical_and(core == 1, xi == third)))
        def _(third=third):
            pltpu.make_async_remote_copy(
                src_ref=fin.at[third], dst_ref=fin.at[third], send_sem=tsend.at[0], recv_sem=frecv.at[third],
                device_id=sibling, device_id_type=MESH,
            ).wait_recv()

        lanes = slice(third * LANES, (third + 1) * LANES)
        bary_ref[:, lanes] = fin[third, 0:32, :]
        pot_ref[lanes] = ENTROPY * wown[lanes] + (norm[:, lanes] - ENTROPY * fin[third, 32:33, :]).reshape(LANES)

    def wait_sent(ref, sem):
        pltpu.make_async_remote_copy(
            src_ref=ref, dst_ref=ref, send_sem=sem, recv_sem=crecv.at[0], device_id=sibling, device_id_type=MESH
        ).wait_send()

    wait_sent(craw.at[pl.ds(0, NZ - 1)], csend.at[0])
    wait_sent(craw.at[pl.ds(0, NZ)], fsend.at[0])
    keeps = jnp.logical_and(home, owner)

    @pl.when(keeps)
    def _():
        wait_sent(pout.at[pl.ds(0, BLOCKS * OWNERS - 1)], psend.at[0])

    @pl.when(jnp.logical_not(keeps))
    def _():
        wait_sent(pout, psend.at[0])

    @pl.when(home)
    def _():
        for e in NEAR + FAR:
            row_copy(e).wait_send()

    @pl.when(jnp.logical_not(home))
    def _():
        last_row_copy().wait_send()

    @pl.when(owner)
    def _():
        wait_sent(pin.at[pl.ds(0, NX * CORES - 1)], tsend.at[0])


def hand_over(pot_in, bary_in, pot_out, bary_out):
    pot_out[...] = pot_in[...]
    bary_out[...] = bary_in[...]


def on_device(src_points, src_logw, tgt_points, tgt_potential, tgt_logw):
    dma = pltpu.SemaphoreType.DMA
    vmem = pltpu.VMEM
    shapes = (jax.ShapeDtypeStruct((ROWS,), F32), jax.ShapeDtypeStruct((DIMS, ROWS), F32))
    results = pl.pallas_call(
        kernel,
        out_shape=shapes,
        in_specs=[pl.BlockSpec(memory_space=pl.ANY)] * 5,
        out_specs=(pl.BlockSpec(memory_space=vmem),) * 2,
        scratch_shapes=[
            vmem((DIMS, ROWS), F32),
            vmem((ROWS,), F32),
            vmem((DIMS, COLS), F32),
            vmem((1, COLS), F32),
            vmem((1, COLS), F32),
            vmem((BLOCKS, DIMS, ROWS), F32),
            vmem((SHARDS, COL_TALL, LANES), F32),
            vmem((SHARDS * COLS, DEPTH), BF16),
            vmem((80, SHARDS * COLS), BF16),
            vmem((DEPTH, BLOCKS * ROWS), BF16),
            vmem((REST, TILE), F32),
            vmem((REST, TILE), F32),
            vmem((8, TILE), F32),
            vmem((8, TILE), F32),
            vmem((8, BLOCKS * ROWS), F32),
            vmem((80, BLOCKS * ROWS), F32),
            vmem((BLOCKS * OWNERS, PIECE_TALL, LANES), F32),
            vmem((NX * NY, PIECE_TALL, LANES), F32),
            vmem((OWNERS, PIECE_TALL, LANES), F32),
            dma((5,)),
            dma((SHARDS,)),
            dma((1,)),
            dma((1,)),
            dma((BLOCKS,)),
            dma((NY,)),
            dma((1,)),
            dma((1,)),
            dma((OWNERS,)),
            dma((1,)),
            pltpu.SemaphoreType.REGULAR,
            pltpu.SemaphoreType.REGULAR,
            pltpu.SemaphoreType.REGULAR,
        ],
        compiler_params=pltpu.CompilerParams(
            collective_id=0, has_side_effects=True, vmem_limit_bytes=63 * 2**20
        ),
    )(src_points, src_logw, tgt_points, tgt_potential, tgt_logw)
    return pl.pallas_call(
        hand_over,
        out_shape=shapes,
        in_specs=[pl.BlockSpec(memory_space=vmem)] * 2,
        out_specs=(pl.BlockSpec(memory_space=vmem),) * 2,
    )(*results)


def solution(mesh):
    return jax.shard_map(
        on_device,
        mesh=mesh,
        in_specs=(
            P(None, "src"),
            P("src"),
            P(None, ("tgt", "src")),
            P(None, ("tgt", "src")),
            P(None, ("tgt", "src")),
        ),
        out_specs=(P("src"), P(None, "src")),
        check_vma=False,
    )
```

```python
import functools
import math

import jax
import jax.numpy as jnp
from jax import lax
from jax.experimental import pallas as pl
from jax.experimental.pallas import tpu as pltpu
from jax.sharding import PartitionSpec as P

ENTROPY = 4.0
LOG2E = math.log2(math.e)
LN2 = math.log(2.0)
MESH = pl.DeviceIdType.MESH
BF16, F32 = jnp.bfloat16, jnp.float32

NY, NZ, NX, CORES = 8, 8, 4, 2
DIMS, ROWS, COLS = 32, 384, 256
TILE = 256
SHARDS = NZ * CORES
BLOCKS = NY // CORES
TILES = BLOCKS * ROWS // TILE
DEPTH = 256
LANES = 128
COL_TALL = 72
PIECE_TALL = 40
OWNERS = ROWS // LANES

COLUMNS = (0, 8, 1, 2, 9, 10, 3, 11, 7, 6, 5, 4, 15, 14, 13, 12)
GROUPS = (4, 3, 5, 4)
SPOT = {place: spot for spot, place in enumerate(COLUMNS)}
LOW = 4

NEAR = (1, 7)
FAR = (2, 6, 3, 5)

EVEN = (4, 2, 6, 0)
ODD = (3, 5, 1, 7)


def split(value):
    first = value.astype(BF16)
    rest = value - first.astype(F32)
    second = rest.astype(BF16)
    third = (rest - second.astype(F32)).astype(BF16)
    return first, second, third


def kernel(
    x_hbm, w_hbm, y_hbm, g_hbm, l_hbm, pot_ref, bary_ref,
    xown, wown, yown, gown, lown, xraw, craw, ya, yw, xa, s0, s1, m0, m1, mrun, acc, pout, pin, fin,
    in_sem, crecv, csend, fsend, rrecv, rsend, precv, psend, frecv, tsend, ready, ready_two, later_in, aside,
):
    loads = [
        pltpu.make_async_copy(a, b, in_sem.at[i])
        for i, (a, b) in enumerate(((x_hbm, xown), (y_hbm, yown), (g_hbm, gown), (l_hbm, lown), (w_hbm, wown)))
    ]
    for load in loads:
        load.start()
    src, tgt = lax.axis_index("src"), lax.axis_index("tgt")
    yi, zi = src // NZ, src % NZ
    xi, core = tgt // CORES, tgt % CORES
    odd = (yi + core) % 2
    home = odd == 0
    low = zi < LOW
    high = jnp.logical_not(low)
    owner = jnp.logical_and(core == 1, xi < OWNERS)

    def y_peer(e):
        return (((yi + e) % NY) * NZ + zi, tgt)

    def z_peer(tie):
        bits = [(zi // 2**i) % 2 for i in range(3)]
        z = sum((1 - bit if tie // 2**i % 2 else bit) * 2**i for i, bit in enumerate(bits))
        return (yi * NZ + z, tgt)

    def x_peer(e):
        return (src, ((xi + e) % NX) * CORES + core)

    def t_peer(e):
        return (src, (tgt + e) % (NX * CORES))

    sibling = (src, xi * CORES + 1 - core)

    barrier = pltpu.get_barrier_semaphore()

    ear = jnp.where(low, core, 1)

    def greet(device, at):
        where, chip_core = device
        there = (where, (chip_core // CORES) * CORES + at)
        pl.semaphore_signal(barrier, inc=1, device_id=there, device_id_type=MESH)

    @pl.when(low)
    def _():
        for tie in range(LOW, NZ):
            greet(z_peer(tie), 0)

    for tie in (3, 2, 1):
        greet(z_peer(tie), ear)
    for e in reversed(NEAR + FAR):
        if e % 2:
            greet(y_peer(e), ear)
        else:

            @pl.when(home)
            def _(e=e):
                greet(y_peer(e), ear)

    for e in (1, NX - 1):
        greet(x_peer(e), ear)
    greet(sibling, 1 - core)

    mrun[...] = jnp.full_like(mrun, -1e30)
    acc[...] = jnp.zeros_like(acc)
    for load in loads:
        load.wait()

    y = yown[...]
    bias = (gown[...] - 0.5 * jnp.sum(y * y, axis=0, keepdims=True)) * (LOG2E / ENTROPY) + lown[...] * LOG2E
    for half in range(2):
        lanes = slice(half * LANES, (half + 1) * LANES)
        craw[0, half * DIMS : (half + 1) * DIMS, :] = y[:, lanes]
    craw[0, 64:72, :] = jnp.concatenate(
        [bias[:, :LANES], bias[:, LANES:], jnp.zeros((6, LANES), F32)], axis=0
    )

    @pl.when(home)
    def _():
        xraw[3] = xown[...]

    @pl.when(low)
    def _():
        pl.semaphore_wait(barrier, 12 - 2 * odd)

    @pl.when(jnp.logical_and(high, core == 0))
    def _():
        pl.semaphore_wait(barrier, 9)

    def column_copy(tie):
        return pltpu.make_async_remote_copy(
            src_ref=craw.at[0], dst_ref=craw.at[tie], send_sem=csend.at[0], recv_sem=crecv.at[tie],
            device_id=z_peer(tie), device_id_type=MESH,
        )

    def pass_copy(tie):
        return pltpu.make_async_remote_copy(
            src_ref=craw.at[tie], dst_ref=craw.at[NZ + tie], send_sem=fsend.at[0],
            recv_sem=crecv.at[NZ + tie], device_id=sibling, device_id_type=MESH,
        )

    def row_copy(e):
        back = (8 - e) % 8
        slot = EVEN.index(back) if back % 2 == 0 else ODD.index(back)
        return pltpu.make_async_remote_copy(
            src_ref=xown, dst_ref=xraw.at[slot], send_sem=rsend.at[e], recv_sem=rrecv.at[slot],
            device_id=y_peer(e), device_id_type=MESH,
        )

    def last_row_copy():
        return pltpu.make_async_remote_copy(
            src_ref=xraw.at[0], dst_ref=xraw.at[0], send_sem=rsend.at[4], recv_sem=rrecv.at[0],
            device_id=y_peer(7), device_id_type=MESH,
        )

    def send_rows(places):
        @pl.when(home)
        def _():
            for e in places:
                row_copy(e).start()

    def across():
        for tie in range(LOW, NZ):
            column_copy(tie).start()

    def wait_column(place):
        pltpu.make_async_remote_copy(
            src_ref=craw.at[place], dst_ref=craw.at[place], send_sem=csend.at[0], recv_sem=crecv.at[place],
            device_id=sibling, device_id_type=MESH,
        ).wait_recv()

    def take(*ties):
        for tie in ties:
            wait_column(tie)
            pass_copy(tie).start()

    def wait_rows(slot):
        pltpu.make_async_remote_copy(
            src_ref=xraw.at[slot], dst_ref=xraw.at[slot], send_sem=rsend.at[0], recv_sem=rrecv.at[slot],
            device_id=sibling, device_id_type=MESH,
        ).wait_recv()

    def prepare_rows(slot):
        x1, x2, x3 = split(xraw[slot] * (LOG2E / ENTROPY))
        row = lax.broadcasted_iota(jnp.int32, (64, ROWS), 0)
        ones = jnp.where(row < 3, 1.0, 0.0).astype(BF16)
        xa[:, slot * ROWS : (slot + 1) * ROWS] = jnp.concatenate([x1, x1, x2, x2, x1, x3, ones], axis=0)

    def prepare_columns(place):
        raw = craw[place]
        y1, y2, y3 = split(jnp.concatenate([raw[:32], raw[32:64]], axis=1))
        b = jnp.concatenate([raw[64:65], raw[65:66]], axis=1)
        b1 = b.astype(BF16).astype(F32)
        b2 = (b - b1).astype(BF16).astype(F32)
        b3 = b - b1 - b2
        row = lax.broadcasted_iota(jnp.int32, (64, COLS), 0)
        biases = jnp.where(row == 0, b1, jnp.where(row == 1, b2, jnp.where(row == 2, b3, 0.0))).astype(BF16)
        deep = jnp.concatenate([y1, y2, y1, y2, y3, y1, biases], axis=0)
        first = SPOT[place] * COLS
        ya[pl.ds(first, COLS), :] = deep.T
        yw[:, pl.ds(first, COLS)] = jnp.concatenate([y1, jnp.ones((16, COLS), BF16), y2], axis=0)

    def tile_lanes(tile):
        return pl.ds(pl.multiple_of(tile * TILE, TILE), TILE)

    def scores(first, span, tile, s, m):
        value = jnp.dot(ya[pl.ds(first, span), :], xa[:, tile_lanes(tile)], preferred_element_type=F32)
        s[0:span, :] = value
        m[...] = jnp.max(value.reshape(span // 8, 8, TILE), axis=0)

    def absorb(first, span, tile, s, m):
        lanes = tile_lanes(tile)
        old = mrun[0:1, lanes]
        new = jnp.maximum(old, jnp.max(m[...], axis=0, keepdims=True))
        mrun[0:1, lanes] = new
        share = jnp.exp2(s[0:span, :] - new)
        high = share.astype(BF16)
        low = (share - high.astype(F32)).astype(BF16)
        sums = jnp.dot(yw[:, pl.ds(first, span)], high, preferred_element_type=F32)
        rest = jnp.dot(yw[0:48, pl.ds(first, span)], low, preferred_element_type=F32)
        sums = jnp.concatenate([sums[:48] + rest, sums[48:]], axis=0)
        acc[:, lanes] = acc[:, lanes] * jnp.exp2(old - new) + sums

    def block_offset(block):
        return EVEN[block] + odd * (ODD[block] - EVEN[block])

    def piece_copy(block, third):
        offset = block_offset(block)
        place = xi * NY + (NY - offset) % NY
        return pltpu.make_async_remote_copy(
            src_ref=pout.at[block * OWNERS + third], dst_ref=pin.at[place],
            send_sem=psend.at[0], recv_sem=precv.at[0],
            device_id=(((yi + offset) % NY) * NZ + zi, third * CORES + 1), device_id_type=MESH,
        )

    def put_piece(ref, index, block, third):
        lanes = slice(block * ROWS + third * LANES, block * ROWS + (third + 1) * LANES)
        ref[index, 0:32, :] = acc[0:32, lanes] + acc[48:80, lanes]
        ref[index, 32:40, :] = jnp.concatenate(
            [acc[32:33, lanes], mrun[0:1, lanes], jnp.zeros((6, LANES), F32)], axis=0
        )

    def stays(block, third):
        return jnp.logical_and(jnp.logical_and(home, core == 1), xi == third)

    def finish_tile(tile):
        for unit in range(tile * TILE // LANES, (tile + 1) * TILE // LANES):
            block, third = unit // OWNERS, unit % OWNERS
            put_piece(pout, unit, block, third)
            if block < 3:
                piece_copy(block, third).start()
            else:

                @pl.when(stays(block, third))
                def _(unit=unit):
                    pltpu.make_async_copy(pout.at[unit], pin.at[xi * NY], precv.at[0]).start()

                @pl.when(jnp.logical_not(stays(block, third)))
                def _(block=block, third=third):
                    piece_copy(block, third).start()

    def prepare(*places):
        for place in places:
            prepare_columns(place)

    def arrived(*ties):
        for tie in ties:
            wait_column(NZ + tie)

    def take_rows(slot):
        wait_rows(slot)
        prepare_rows(slot)

    def tell_sibling():
        pl.semaphore_signal(aside, inc=1, device_id=sibling, device_id_type=MESH)

    @pl.when(jnp.logical_and(high, core == 0))
    def _():
        tell_sibling()

    @pl.when(jnp.logical_and(high, core == 1))
    def _():
        pl.semaphore_wait(aside, 1)

    @pl.when(high)
    def _():
        across()
        for tie in range(LOW, NZ):
            pl.semaphore_signal(later_in, inc=1, device_id=z_peer(tie), device_id_type=MESH)

    @pl.when(jnp.logical_and(high, core == 1))
    def _():
        pl.semaphore_wait(barrier, 21)
        tell_sibling()

    @pl.when(jnp.logical_and(high, core == 0))
    def _():
        pl.semaphore_wait(aside, 1)

    pass_copy(0).start()
    column_copy(1).start()
    send_rows(NEAR)
    column_copy(2).start()
    prepare(0)

    @pl.when(home)
    def _():
        prepare_rows(3)

    column_copy(3).start()
    send_rows(FAR)

    @pl.when(jnp.logical_not(home))
    def _():
        take_rows(3)

    arrived(0)
    take(1, 2)
    prepare(8, 1, 2)

    buffers = ((s0, m0), (s1, m1))

    def step(number, done, following):
        if following is not None:
            scores(*following, *buffers[(number + 1) % 2])
        if done is not None:
            absorb(*done, *buffers[number % 2])

    one, two, three, rest = ((COLS * sum(GROUPS[:i]), COLS * GROUPS[i]) for i in range(4))

    step(-1, None, (*one, 5))
    take_rows(2)
    step(0, (*one, 5), (*one, 4))
    step(1, (*one, 4), (*one, 3))
    take_rows(1)

    @pl.when(jnp.logical_not(home))
    def _():
        wait_rows(0)
        last_row_copy().start()
        prepare_rows(0)

    @pl.when(low)
    def _():
        pl.semaphore_wait(later_in, NZ - LOW)
        across()

    step(2, (*one, 3), (*one, 2))
    arrived(1, 2)
    take(3)
    prepare(9, 10, 3)
    step(3, (*one, 2), (*two, 5))

    step(4, (*two, 5), (*two, 4))
    step(5, (*two, 4), (*two, 3))
    step(6, (*two, 3), (*two, 2))

    @pl.when(home)
    def _():
        take_rows(0)

    for e in (1, NX - 1):
        pl.semaphore_signal(ready, inc=1, device_id=x_peer(e), device_id_type=MESH)
    step(7, (*two, 2), (*one, 1))
    step(8, (*one, 1), (*one, 0))
    step(9, (*one, 0), (*two, 1))
    step(10, (*two, 1), (*two, 0))
    take(7, 6, 5, 4)
    arrived(3)
    prepare(11, 7, 6, 5, 4)
    step(11, (*two, 0), (*three, 0))
    pl.semaphore_wait(ready, 2)
    for e in (1, NX - 1):
        pl.semaphore_signal(ready_two, inc=1, device_id=x_peer(e), device_id_type=MESH)
    step(12, (*three, 0), (*three, 1))
    step(13, (*three, 1), (*three, 2))
    arrived(7, 6, 5, 4)
    prepare(15, 14, 13, 12)
    step(14, (*three, 2), (*rest, 0))

    step(15, (*rest, 0), (*three, 3))
    pl.semaphore_wait(ready_two, 2)
    finish_tile(0)
    step(16, (*three, 3), (*rest, 1))
    step(17, (*rest, 1), (*three, 4))
    finish_tile(1)
    step(18, (*three, 4), (*rest, 2))
    step(19, (*rest, 2), (*three, 5))
    finish_tile(2)
    step(20, (*three, 5), (*rest, 3))
    step(21, (*rest, 3), (*rest, 4))
    finish_tile(3)
    step(22, (*rest, 4), (*rest, 5))
    finish_tile(4)
    step(23, (*rest, 5), None)
    finish_tile(5)

    def result_copy(e):
        return pltpu.make_async_remote_copy(
            src_ref=fin.at[xi], dst_ref=fin.at[xi], send_sem=tsend.at[0], recv_sem=frecv.at[xi],
            device_id=t_peer(e), device_id_type=MESH,
        )

    @pl.when(owner)
    def _():
        pltpu.make_async_copy(pin, pin, precv.at[0]).wait()
        places = range(NX * NY)
        tops = [pin[place, 32:40, :] for place in places]
        peak = functools.reduce(jnp.maximum, tops)[1:2]
        factors = [jnp.exp2(top[1:2] - peak) for top in tops]
        total = functools.reduce(jnp.add, [top[0:1] * f for top, f in zip(tops, factors, strict=True)])
        weighted = functools.reduce(
            jnp.add, [pin[place, 0:32, :] * f for place, f in zip(places, factors, strict=True)]
        )
        fin[xi, 0:32, :] = weighted / total
        fin[xi, 32:40, :] = jnp.broadcast_to(peak * LN2 + jnp.log(total), (8, LANES))
        for e in (4, 3, 5, 2, 6, 1, 7):
            result_copy(e).start()

    x = xown[...]
    norm = 0.5 * jnp.sum(x * x, axis=0, keepdims=True)
    for third in range(OWNERS):

        @pl.when(jnp.logical_not(jnp.logical_and(core == 1, xi == third)))
        def _(third=third):
            pltpu.make_async_remote_copy(
                src_ref=fin.at[third], dst_ref=fin.at[third], send_sem=tsend.at[0], recv_sem=frecv.at[third],
                device_id=sibling, device_id_type=MESH,
            ).wait_recv()

        lanes = slice(third * LANES, (third + 1) * LANES)
        bary_ref[:, lanes] = fin[third, 0:32, :]
        pot_ref[lanes] = ENTROPY * wown[lanes] + (norm[:, lanes] - ENTROPY * fin[third, 32:33, :]).reshape(LANES)

    def wait_sent(ref, sem):
        pltpu.make_async_remote_copy(
            src_ref=ref, dst_ref=ref, send_sem=sem, recv_sem=crecv.at[0], device_id=sibling, device_id_type=MESH
        ).wait_send()

    wait_sent(craw.at[pl.ds(0, NZ - 1)], csend.at[0])
    wait_sent(craw.at[pl.ds(0, NZ)], fsend.at[0])
    keeps = jnp.logical_and(home, owner)

    @pl.when(keeps)
    def _():
        wait_sent(pout.at[pl.ds(0, BLOCKS * OWNERS - 1)], psend.at[0])

    @pl.when(jnp.logical_not(keeps))
    def _():
        wait_sent(pout, psend.at[0])

    @pl.when(home)
    def _():
        for e in NEAR + FAR:
            row_copy(e).wait_send()

    @pl.when(jnp.logical_not(home))
    def _():
        last_row_copy().wait_send()

    @pl.when(owner)
    def _():
        wait_sent(pin.at[pl.ds(0, NX * CORES - 1)], tsend.at[0])


def hand_over(pot_in, bary_in, pot_out, bary_out):
    pot_out[...] = pot_in[...]
    bary_out[...] = bary_in[...]


def on_device(src_points, src_logw, tgt_points, tgt_potential, tgt_logw):
    dma = pltpu.SemaphoreType.DMA
    vmem = pltpu.VMEM
    shapes = (jax.ShapeDtypeStruct((ROWS,), F32), jax.ShapeDtypeStruct((DIMS, ROWS), F32))
    results = pl.pallas_call(
        kernel,
        out_shape=shapes,
        in_specs=[pl.BlockSpec(memory_space=pl.ANY)] * 5,
        out_specs=(pl.BlockSpec(memory_space=vmem),) * 2,
        scratch_shapes=[
            vmem((DIMS, ROWS), F32),
            vmem((ROWS,), F32),
            vmem((DIMS, COLS), F32),
            vmem((1, COLS), F32),
            vmem((1, COLS), F32),
            vmem((BLOCKS, DIMS, ROWS), F32),
            vmem((SHARDS, COL_TALL, LANES), F32),
            vmem((SHARDS * COLS, DEPTH), BF16),
            vmem((80, SHARDS * COLS), BF16),
            vmem((DEPTH, BLOCKS * ROWS), BF16),
            vmem((COLS * max(GROUPS), TILE), F32),
            vmem((COLS * max(GROUPS), TILE), F32),
            vmem((8, TILE), F32),
            vmem((8, TILE), F32),
            vmem((8, BLOCKS * ROWS), F32),
            vmem((80, BLOCKS * ROWS), F32),
            vmem((BLOCKS * OWNERS, PIECE_TALL, LANES), F32),
            vmem((NX * NY, PIECE_TALL, LANES), F32),
            vmem((OWNERS, PIECE_TALL, LANES), F32),
            dma((5,)),
            dma((SHARDS,)),
            dma((1,)),
            dma((1,)),
            dma((BLOCKS,)),
            dma((NY,)),
            dma((1,)),
            dma((1,)),
            dma((OWNERS,)),
            dma((1,)),
            pltpu.SemaphoreType.REGULAR,
            pltpu.SemaphoreType.REGULAR,
            pltpu.SemaphoreType.REGULAR,
            pltpu.SemaphoreType.REGULAR,
        ],
        compiler_params=pltpu.CompilerParams(
            collective_id=0, has_side_effects=True, vmem_limit_bytes=63 * 2**20
        ),
    )(src_points, src_logw, tgt_points, tgt_potential, tgt_logw)
    return pl.pallas_call(
        hand_over,
        out_shape=shapes,
        in_specs=[pl.BlockSpec(memory_space=vmem)] * 2,
        out_specs=(pl.BlockSpec(memory_space=vmem),) * 2,
    )(*results)


def solution(mesh):
    return jax.shard_map(
        on_device,
        mesh=mesh,
        in_specs=(
            P(None, "src"),
            P("src"),
            P(None, ("tgt", "src")),
            P(None, ("tgt", "src")),
            P(None, ("tgt", "src")),
        ),
        out_specs=(P("src"), P(None, "src")),
        check_vma=False,
    )
```

```python
import functools
import math

import jax
import jax.numpy as jnp
from jax import lax
from jax.experimental import pallas as pl
from jax.experimental.pallas import tpu as pltpu
from jax.sharding import PartitionSpec as P

ENTROPY = 4.0
LOG2E = math.log2(math.e)
LN2 = math.log(2.0)
MESH = pl.DeviceIdType.MESH
BF16, F32 = jnp.bfloat16, jnp.float32

NY, NZ, NX, CORES = 8, 8, 4, 2
DIMS, ROWS, COLS = 32, 384, 256
TILE = 256
SHARDS = NZ * CORES
BLOCKS = NY // CORES
TILES = BLOCKS * ROWS // TILE
DEPTH = 256
LANES = 128
COL_TALL = 72
PIECE_TALL = 40
OWNERS = ROWS // LANES

COLUMNS = (0, 8, 1, 2, 9, 10, 3, 11, 7, 6, 5, 4, 15, 14, 13, 12)
GROUPS = (4, 3, 5, 4)
SPOT = {place: spot for spot, place in enumerate(COLUMNS)}
LOW = 4

NEAR = (1, 7)
FAR = (2, 6, 3, 5)

EVEN = (4, 2, 6, 0)
ODD = (3, 5, 1, 7)


def split(value):
    first = value.astype(BF16)
    rest = value - first.astype(F32)
    second = rest.astype(BF16)
    third = (rest - second.astype(F32)).astype(BF16)
    return first, second, third


def kernel(
    x_hbm, w_hbm, y_hbm, g_hbm, l_hbm, pot_ref, bary_ref,
    xown, wown, yown, gown, lown, xraw, craw, ya, yw, xa, s0, s1, m0, m1, mrun, acc, pout, pin, fin,
    in_sem, crecv, csend, fsend, rrecv, rsend, precv, psend, frecv, tsend, ready, ready_two, later_in, aside,
):
    loads = [
        pltpu.make_async_copy(a, b, in_sem.at[i])
        for i, (a, b) in enumerate(((x_hbm, xown), (y_hbm, yown), (g_hbm, gown), (l_hbm, lown), (w_hbm, wown)))
    ]
    for load in loads:
        load.start()
    src, tgt = lax.axis_index("src"), lax.axis_index("tgt")
    yi, zi = src // NZ, src % NZ
    xi, core = tgt // CORES, tgt % CORES
    odd = (yi + core) % 2
    home = odd == 0
    low = zi < LOW
    high = jnp.logical_not(low)
    owner = jnp.logical_and(core == 1, xi < OWNERS)

    def y_peer(e):
        return (((yi + e) % NY) * NZ + zi, tgt)

    def z_peer(tie):
        bits = [(zi // 2**i) % 2 for i in range(3)]
        z = sum((1 - bit if tie // 2**i % 2 else bit) * 2**i for i, bit in enumerate(bits))
        return (yi * NZ + z, tgt)

    def x_peer(e):
        return (src, ((xi + e) % NX) * CORES + core)

    def t_peer(e):
        return (src, (tgt + e) % (NX * CORES))

    sibling = (src, xi * CORES + 1 - core)

    barrier = pltpu.get_barrier_semaphore()

    ear = jnp.where(low, core, 1)

    def greet(device, at):
        where, chip_core = device
        there = (where, (chip_core // CORES) * CORES + at)
        pl.semaphore_signal(barrier, inc=1, device_id=there, device_id_type=MESH)

    @pl.when(low)
    def _():
        for tie in range(LOW, NZ):
            greet(z_peer(tie), 0)

    for tie in (3, 2, 1):
        greet(z_peer(tie), ear)
    for e in reversed(NEAR + FAR):
        if e % 2:
            greet(y_peer(e), ear)
        else:

            @pl.when(home)
            def _(e=e):
                greet(y_peer(e), ear)

    for e in (1, NX - 1):
        greet(x_peer(e), ear)
    greet(sibling, 1 - core)

    mrun[...] = jnp.full_like(mrun, -1e30)
    acc[...] = jnp.zeros_like(acc)
    for load in loads:
        load.wait()

    y = yown[...]
    bias = (gown[...] - 0.5 * jnp.sum(y * y, axis=0, keepdims=True)) * (LOG2E / ENTROPY) + lown[...] * LOG2E
    for half in range(2):
        lanes = slice(half * LANES, (half + 1) * LANES)
        craw[0, half * DIMS : (half + 1) * DIMS, :] = y[:, lanes]
    craw[0, 64:72, :] = jnp.concatenate(
        [bias[:, :LANES], bias[:, LANES:], jnp.zeros((6, LANES), F32)], axis=0
    )

    @pl.when(home)
    def _():
        xraw[3] = xown[...]

    @pl.when(low)
    def _():
        pl.semaphore_wait(barrier, 12 - 2 * odd)

    @pl.when(jnp.logical_and(high, core == 0))
    def _():
        pl.semaphore_wait(barrier, 9)

    def column_copy(tie):
        return pltpu.make_async_remote_copy(
            src_ref=craw.at[0], dst_ref=craw.at[tie], send_sem=csend.at[0], recv_sem=crecv.at[tie],
            device_id=z_peer(tie), device_id_type=MESH,
        )

    def pass_copy(tie):
        return pltpu.make_async_remote_copy(
            src_ref=craw.at[tie], dst_ref=craw.at[NZ + tie], send_sem=fsend.at[0],
            recv_sem=crecv.at[NZ + tie], device_id=sibling, device_id_type=MESH,
        )

    def early_copy(z):
        tie = sum(((zi // 2**i) % 2 + (1 - 2 * ((zi // 2**i) % 2)) * (z // 2**i % 2)) * 2**i for i in range(3))
        return pltpu.make_async_remote_copy(
            src_ref=craw.at[0], dst_ref=craw.at[tie], send_sem=csend.at[0], recv_sem=crecv.at[tie],
            device_id=(yi * NZ + z, tgt), device_id_type=MESH,
        )

    def row_copy(e):
        back = (8 - e) % 8
        slot = EVEN.index(back) if back % 2 == 0 else ODD.index(back)
        return pltpu.make_async_remote_copy(
            src_ref=xown, dst_ref=xraw.at[slot], send_sem=rsend.at[e], recv_sem=rrecv.at[slot],
            device_id=y_peer(e), device_id_type=MESH,
        )

    def last_row_copy():
        return pltpu.make_async_remote_copy(
            src_ref=xraw.at[0], dst_ref=xraw.at[0], send_sem=rsend.at[4], recv_sem=rrecv.at[0],
            device_id=y_peer(7), device_id_type=MESH,
        )

    def send_rows(places):
        @pl.when(home)
        def _():
            for e in places:
                row_copy(e).start()

    def across():
        for tie in range(LOW, NZ):
            column_copy(tie).start()

    def wait_column(place):
        pltpu.make_async_remote_copy(
            src_ref=craw.at[place], dst_ref=craw.at[place], send_sem=csend.at[0], recv_sem=crecv.at[place],
            device_id=sibling, device_id_type=MESH,
        ).wait_recv()

    def take(*ties):
        for tie in ties:
            wait_column(tie)
            pass_copy(tie).start()

    def wait_rows(slot):
        pltpu.make_async_remote_copy(
            src_ref=xraw.at[slot], dst_ref=xraw.at[slot], send_sem=rsend.at[0], recv_sem=rrecv.at[slot],
            device_id=sibling, device_id_type=MESH,
        ).wait_recv()

    def prepare_rows(slot):
        x1, x2, x3 = split(xraw[slot] * (LOG2E / ENTROPY))
        row = lax.broadcasted_iota(jnp.int32, (64, ROWS), 0)
        ones = jnp.where(row < 3, 1.0, 0.0).astype(BF16)
        xa[:, slot * ROWS : (slot + 1) * ROWS] = jnp.concatenate([x1, x1, x2, x2, x1, x3, ones], axis=0)

    def prepare_columns(place):
        raw = craw[place]
        y1, y2, y3 = split(jnp.concatenate([raw[:32], raw[32:64]], axis=1))
        b = jnp.concatenate([raw[64:65], raw[65:66]], axis=1)
        b1 = b.astype(BF16).astype(F32)
        b2 = (b - b1).astype(BF16).astype(F32)
        b3 = b - b1 - b2
        row = lax.broadcasted_iota(jnp.int32, (64, COLS), 0)
        biases = jnp.where(row == 0, b1, jnp.where(row == 1, b2, jnp.where(row == 2, b3, 0.0))).astype(BF16)
        deep = jnp.concatenate([y1, y2, y1, y2, y3, y1, biases], axis=0)
        first = SPOT[place] * COLS
        ya[pl.ds(first, COLS), :] = deep.T
        yw[:, pl.ds(first, COLS)] = jnp.concatenate([y1, jnp.ones((16, COLS), BF16), y2], axis=0)

    def tile_lanes(tile):
        return pl.ds(pl.multiple_of(tile * TILE, TILE), TILE)

    def scores(first, span, tile, s, m):
        value = jnp.dot(ya[pl.ds(first, span), :], xa[:, tile_lanes(tile)], preferred_element_type=F32)
        s[0:span, :] = value
        m[...] = jnp.max(value.reshape(span // 8, 8, TILE), axis=0)

    def absorb(first, span, tile, s, m):
        lanes = tile_lanes(tile)
        old = mrun[0:1, lanes]
        new = jnp.maximum(old, jnp.max(m[...], axis=0, keepdims=True))
        mrun[0:1, lanes] = new
        share = jnp.exp2(s[0:span, :] - new)
        high = share.astype(BF16)
        low = (share - high.astype(F32)).astype(BF16)
        sums = jnp.dot(yw[:, pl.ds(first, span)], high, preferred_element_type=F32)
        rest = jnp.dot(yw[0:48, pl.ds(first, span)], low, preferred_element_type=F32)
        sums = jnp.concatenate([sums[:48] + rest, sums[48:]], axis=0)
        acc[:, lanes] = acc[:, lanes] * jnp.exp2(old - new) + sums

    def block_offset(block):
        return EVEN[block] + odd * (ODD[block] - EVEN[block])

    def piece_copy(block, third):
        offset = block_offset(block)
        place = xi * NY + (NY - offset) % NY
        return pltpu.make_async_remote_copy(
            src_ref=pout.at[block * OWNERS + third], dst_ref=pin.at[place],
            send_sem=psend.at[0], recv_sem=precv.at[0],
            device_id=(((yi + offset) % NY) * NZ + zi, third * CORES + 1), device_id_type=MESH,
        )

    def put_piece(ref, index, block, third):
        lanes = slice(block * ROWS + third * LANES, block * ROWS + (third + 1) * LANES)
        ref[index, 0:32, :] = acc[0:32, lanes] + acc[48:80, lanes]
        ref[index, 32:40, :] = jnp.concatenate(
            [acc[32:33, lanes], mrun[0:1, lanes], jnp.zeros((6, LANES), F32)], axis=0
        )

    def stays(block, third):
        return jnp.logical_and(jnp.logical_and(home, core == 1), xi == third)

    def finish_tile(tile):
        for unit in range(tile * TILE // LANES, (tile + 1) * TILE // LANES):
            block, third = unit // OWNERS, unit % OWNERS
            put_piece(pout, unit, block, third)
            if block < 3:
                piece_copy(block, third).start()
            else:

                @pl.when(stays(block, third))
                def _(unit=unit):
                    pltpu.make_async_copy(pout.at[unit], pin.at[xi * NY], precv.at[0]).start()

                @pl.when(jnp.logical_not(stays(block, third)))
                def _(block=block, third=third):
                    piece_copy(block, third).start()

    def prepare(*places):
        for place in places:
            prepare_columns(place)

    def arrived(*ties):
        for tie in ties:
            wait_column(NZ + tie)

    def take_rows(slot):
        wait_rows(slot)
        prepare_rows(slot)

    def tell_sibling():
        pl.semaphore_signal(aside, inc=1, device_id=sibling, device_id_type=MESH)

    @pl.when(jnp.logical_and(high, core == 0))
    def _():
        tell_sibling()

    @pl.when(jnp.logical_and(high, core == 1))
    def _():
        pl.semaphore_wait(aside, 1)

    @pl.when(high)
    def _():
        for z in range(LOW):
            early_copy(z).start()
        for tie in range(LOW, NZ):
            pl.semaphore_signal(later_in, inc=1, device_id=z_peer(tie), device_id_type=MESH)

    @pl.when(jnp.logical_and(high, core == 1))
    def _():
        pl.semaphore_wait(barrier, 21)
        tell_sibling()

    @pl.when(jnp.logical_and(high, core == 0))
    def _():
        pl.semaphore_wait(aside, 1)

    pass_copy(0).start()
    column_copy(1).start()
    send_rows(NEAR)
    column_copy(2).start()
    prepare(0)

    @pl.when(home)
    def _():
        prepare_rows(3)

    column_copy(3).start()
    send_rows(FAR)

    @pl.when(jnp.logical_not(home))
    def _():
        take_rows(3)

    arrived(0)
    take(1, 2)
    prepare(8, 1, 2)

    buffers = ((s0, m0), (s1, m1))

    def step(number, done, following):
        if following is not None:
            scores(*following, *buffers[(number + 1) % 2])
        if done is not None:
            absorb(*done, *buffers[number % 2])

    one, two, three, rest = ((COLS * sum(GROUPS[:i]), COLS * GROUPS[i]) for i in range(4))

    step(-1, None, (*one, 5))
    take_rows(2)
    step(0, (*one, 5), (*one, 4))
    step(1, (*one, 4), (*one, 3))
    take_rows(1)

    @pl.when(jnp.logical_not(home))
    def _():
        wait_rows(0)
        last_row_copy().start()
        prepare_rows(0)

    @pl.when(low)
    def _():
        pl.semaphore_wait(later_in, NZ - LOW)
        across()

    step(2, (*one, 3), (*one, 2))
    arrived(1, 2)
    take(3)
    prepare(9, 10, 3)
    step(3, (*one, 2), (*two, 5))

    step(4, (*two, 5), (*two, 4))
    step(5, (*two, 4), (*two, 3))
    step(6, (*two, 3), (*two, 2))

    @pl.when(home)
    def _():
        take_rows(0)

    for e in (1, NX - 1):
        pl.semaphore_signal(ready, inc=1, device_id=x_peer(e), device_id_type=MESH)
    step(7, (*two, 2), (*one, 1))
    step(8, (*one, 1), (*one, 0))
    step(9, (*one, 0), (*two, 1))
    step(10, (*two, 1), (*two, 0))
    take(7, 6, 5, 4)
    arrived(3)
    prepare(11, 7, 6, 5, 4)
    step(11, (*two, 0), (*three, 0))
    pl.semaphore_wait(ready, 2)
    for e in (1, NX - 1):
        pl.semaphore_signal(ready_two, inc=1, device_id=x_peer(e), device_id_type=MESH)
    step(12, (*three, 0), (*three, 1))
    step(13, (*three, 1), (*three, 2))
    arrived(7, 6, 5, 4)
    prepare(15, 14, 13, 12)
    step(14, (*three, 2), (*rest, 0))

    step(15, (*rest, 0), (*three, 3))
    pl.semaphore_wait(ready_two, 2)
    finish_tile(0)
    step(16, (*three, 3), (*rest, 1))
    step(17, (*rest, 1), (*three, 4))
    finish_tile(1)
    step(18, (*three, 4), (*rest, 2))
    step(19, (*rest, 2), (*three, 5))
    finish_tile(2)
    step(20, (*three, 5), (*rest, 3))
    step(21, (*rest, 3), (*rest, 4))
    finish_tile(3)
    step(22, (*rest, 4), (*rest, 5))
    finish_tile(4)
    step(23, (*rest, 5), None)
    finish_tile(5)

    def result_copy(e):
        return pltpu.make_async_remote_copy(
            src_ref=fin.at[xi], dst_ref=fin.at[xi], send_sem=tsend.at[0], recv_sem=frecv.at[xi],
            device_id=t_peer(e), device_id_type=MESH,
        )

    @pl.when(owner)
    def _():
        pltpu.make_async_copy(pin, pin, precv.at[0]).wait()
        places = range(NX * NY)
        tops = [pin[place, 32:40, :] for place in places]
        peak = functools.reduce(jnp.maximum, tops)[1:2]
        factors = [jnp.exp2(top[1:2] - peak) for top in tops]
        total = functools.reduce(jnp.add, [top[0:1] * f for top, f in zip(tops, factors, strict=True)])
        weighted = functools.reduce(
            jnp.add, [pin[place, 0:32, :] * f for place, f in zip(places, factors, strict=True)]
        )
        fin[xi, 0:32, :] = weighted / total
        fin[xi, 32:40, :] = jnp.broadcast_to(peak * LN2 + jnp.log(total), (8, LANES))
        for e in (4, 3, 5, 2, 6, 1, 7):
            result_copy(e).start()

    x = xown[...]
    norm = 0.5 * jnp.sum(x * x, axis=0, keepdims=True)
    for third in range(OWNERS):

        @pl.when(jnp.logical_not(jnp.logical_and(core == 1, xi == third)))
        def _(third=third):
            pltpu.make_async_remote_copy(
                src_ref=fin.at[third], dst_ref=fin.at[third], send_sem=tsend.at[0], recv_sem=frecv.at[third],
                device_id=sibling, device_id_type=MESH,
            ).wait_recv()

        lanes = slice(third * LANES, (third + 1) * LANES)
        bary_ref[:, lanes] = fin[third, 0:32, :]
        pot_ref[lanes] = ENTROPY * wown[lanes] + (norm[:, lanes] - ENTROPY * fin[third, 32:33, :]).reshape(LANES)

    def wait_sent(ref, sem):
        pltpu.make_async_remote_copy(
            src_ref=ref, dst_ref=ref, send_sem=sem, recv_sem=crecv.at[0], device_id=sibling, device_id_type=MESH
        ).wait_send()

    wait_sent(craw.at[pl.ds(0, NZ - 1)], csend.at[0])
    wait_sent(craw.at[pl.ds(0, NZ)], fsend.at[0])
    keeps = jnp.logical_and(home, owner)

    @pl.when(keeps)
    def _():
        wait_sent(pout.at[pl.ds(0, BLOCKS * OWNERS - 1)], psend.at[0])

    @pl.when(jnp.logical_not(keeps))
    def _():
        wait_sent(pout, psend.at[0])

    @pl.when(home)
    def _():
        for e in NEAR + FAR:
            row_copy(e).wait_send()

    @pl.when(jnp.logical_not(home))
    def _():
        last_row_copy().wait_send()

    @pl.when(owner)
    def _():
        wait_sent(pin.at[pl.ds(0, NX * CORES - 1)], tsend.at[0])


def hand_over(pot_in, bary_in, pot_out, bary_out):
    pot_out[...] = pot_in[...]
    bary_out[...] = bary_in[...]


def on_device(src_points, src_logw, tgt_points, tgt_potential, tgt_logw):
    dma = pltpu.SemaphoreType.DMA
    vmem = pltpu.VMEM
    shapes = (jax.ShapeDtypeStruct((ROWS,), F32), jax.ShapeDtypeStruct((DIMS, ROWS), F32))
    results = pl.pallas_call(
        kernel,
        out_shape=shapes,
        in_specs=[pl.BlockSpec(memory_space=pl.ANY)] * 5,
        out_specs=(pl.BlockSpec(memory_space=vmem),) * 2,
        scratch_shapes=[
            vmem((DIMS, ROWS), F32),
            vmem((ROWS,), F32),
            vmem((DIMS, COLS), F32),
            vmem((1, COLS), F32),
            vmem((1, COLS), F32),
            vmem((BLOCKS, DIMS, ROWS), F32),
            vmem((SHARDS, COL_TALL, LANES), F32),
            vmem((SHARDS * COLS, DEPTH), BF16),
            vmem((80, SHARDS * COLS), BF16),
            vmem((DEPTH, BLOCKS * ROWS), BF16),
            vmem((COLS * max(GROUPS), TILE), F32),
            vmem((COLS * max(GROUPS), TILE), F32),
            vmem((8, TILE), F32),
            vmem((8, TILE), F32),
            vmem((8, BLOCKS * ROWS), F32),
            vmem((80, BLOCKS * ROWS), F32),
            vmem((BLOCKS * OWNERS, PIECE_TALL, LANES), F32),
            vmem((NX * NY, PIECE_TALL, LANES), F32),
            vmem((OWNERS, PIECE_TALL, LANES), F32),
            dma((5,)),
            dma((SHARDS,)),
            dma((1,)),
            dma((1,)),
            dma((BLOCKS,)),
            dma((NY,)),
            dma((1,)),
            dma((1,)),
            dma((OWNERS,)),
            dma((1,)),
            pltpu.SemaphoreType.REGULAR,
            pltpu.SemaphoreType.REGULAR,
            pltpu.SemaphoreType.REGULAR,
            pltpu.SemaphoreType.REGULAR,
        ],
        compiler_params=pltpu.CompilerParams(
            collective_id=0, has_side_effects=True, vmem_limit_bytes=63 * 2**20
        ),
    )(src_points, src_logw, tgt_points, tgt_potential, tgt_logw)
    return pl.pallas_call(
        hand_over,
        out_shape=shapes,
        in_specs=[pl.BlockSpec(memory_space=vmem)] * 2,
        out_specs=(pl.BlockSpec(memory_space=vmem),) * 2,
    )(*results)


def solution(mesh):
    return jax.shard_map(
        on_device,
        mesh=mesh,
        in_specs=(
            P(None, "src"),
            P("src"),
            P(None, ("tgt", "src")),
            P(None, ("tgt", "src")),
            P(None, ("tgt", "src")),
        ),
        out_specs=(P("src"), P(None, "src")),
        check_vma=False,
    )
```
